128 devices in a mesh: dp: 32 (over y, x_lo, z), mp: 4 (over x_hi, core).
Axes of the slice: x: 4 (x_hi: 2, x_lo: 2; x = x_hi * 2 + x_lo), y: 4, z: 4, core: 2. Of those that a mesh axis runs over, the one named last changes fastest.
Arguments:
- tokens: bfloat16 [96, 256, 1024], P('dp', 'mp'), may hold values from -6 to 6
- clear_count: int32 [96, 256], P('dp', 'mp'), may hold values from 0 to 256
- gain_one: float32 [1024], replicated, may hold values from 0.25 to 1.75
- spatial_qkv: bfloat16 [3, 1024, 1024], P(None, None, 'mp'), as said below
- spatial_out: bfloat16 [1024, 1024], P('mp'), may hold values from -0.1875 to 0.1875
- gain_two: float32 [1024], replicated, may hold values from 0.25 to 1.75
- mlp_up: bfloat16 [1024, 4096], P(None, 'mp'), may hold values from -0.1875 to 0.1875
- mlp_down: bfloat16 [4096, 1024], P('mp'), may hold values from -0.09375 to 0.09375
- gain_three: float32 [1024], replicated, may hold values from 0.25 to 1.75
- temporal_qkv: bfloat16 [3, 1024, 1024], replicated, as said below
- temporal_out: bfloat16 [1024, 1024], replicated, may hold values from -0.1875 to 0.1875
Outputs:
- joined: bfloat16 [96, 4, 64, 1024], P(None, 'mp', 'dp')
The draws below stay inside these ranges and needn't reach their ends.
Inputs may be any that keep to these rules, and one draw needn't show every extreme that they name: `spatial_qkv`: each of the three 1024 x 1024 matrices has entries of order 1024^-0.5 times a factor of at most 40; nothing else is promised. `temporal_qkv`: as for spatial_qkv.
All inputs are finite; a program needn't handle non-finite values.
Results may differ from the reference program's by a relative error of at most 0.02.
Values may be sent and summed in bfloat16 or wider, within the bound.
A program may use at most 64 MiB of HBM per device.

```python
import math
import jax
import jax.numpy as jnp
from jax import lax

D = 1024
HEADS = 16
HD = 64
FF = 4096
P_SIZE = 256
PIX = 256
FRAMES = 12
S = 96
TILES = 8
GROUPS = 4
PQ = 64


def projection_law(key):
    base = jax.random.normal(key, (3, D, D), jnp.float32) / math.sqrt(D)
    return base


def draw_spatial_qkv(key, part):
    return projection_law(jax.random.fold_in(key, 11)).astype(jnp.bfloat16)


def draw_temporal_qkv(key, part):
    return projection_law(jax.random.fold_in(key, 23)).astype(jnp.bfloat16)


def plant(drawn, own_key, low, top_value):
    longest = drawn.shape.index(max(drawn.shape))
    spots = []
    for shift in (0, 1):
        where = [jax.random.randint(jax.random.fold_in(own_key, axis), (), 0, length) for axis, length in enumerate(drawn.shape)]
        where[longest] = (where[longest] + shift) % drawn.shape[longest]
        spots.append(tuple(where))
    return drawn.at[spots[0]].set(low).at[spots[1]].set(top_value)


def block_scale(rng, dims, shards, low, largest):
    level, own = 1.0, jax.random.fold_in(rng, 6)
    for position, parts in shards:
        steps = jnp.exp(jax.random.uniform(jax.random.fold_in(own, position), (parts,), jnp.float32, low / len(shards), largest / len(shards)))
        level = level * jnp.repeat(steps, dims[position] // parts).reshape([-1 if axis == position else 1 for axis in range(len(dims))])
    return level


def normal_values(key, dims, deviation, most, pieces=(), dtype=jnp.bfloat16):
    values = deviation * jax.random.normal(key, dims, jnp.float32)
    if pieces:
        values = values * block_scale(key, dims, pieces, -0.22, 0.18)
    return jnp.clip(values, -most, most).astype(dtype)


def setup_inputs(seed: int = 0) -> dict:
    streams_of = jax.random.split(jax.random.key(seed), 12)
    return {
        "tokens": normal_values(streams_of[0], (S, P_SIZE, D), 1.0, 6.0, ((0, 32), (1, 4))),
        "clear_count": plant(jax.random.randint(streams_of[1], (S, P_SIZE), 0, PIX + 1), jax.random.fold_in(streams_of[1], 1), 0, PIX).astype(jnp.int32),
        "gain_one": jnp.clip(1.0 + 0.15 * jax.random.normal(streams_of[2], (D,), jnp.float32), 0.25, 1.75),
        "spatial_qkv": draw_spatial_qkv(jax.random.fold_in(streams_of[11], 71), 0),
        "spatial_out": normal_values(streams_of[4], (D, D), D ** -0.5, 0.1875, ((0, 4),)),
        "gain_two": jnp.clip(1.0 + 0.15 * jax.random.normal(streams_of[5], (D,), jnp.float32), 0.25, 1.75),
        "mlp_up": normal_values(streams_of[6], (D, FF), D ** -0.5, 0.1875, ((1, 4),)),
        "mlp_down": normal_values(streams_of[7], (FF, D), FF ** -0.5, 0.09375, ((0, 4),)),
        "gain_three": jnp.clip(1.0 + 0.15 * jax.random.normal(streams_of[8], (D,), jnp.float32), 0.25, 1.75),
        "temporal_qkv": draw_temporal_qkv(jax.random.fold_in(streams_of[11], 71), 0),
        "temporal_out": normal_values(streams_of[10], (D, D), D ** -0.5, 0.1875),
    }


EPS = 1e-06

def normalize(rows, gain):
    mean = lax.optimization_barrier(jnp.mean(rows, axis=-1, keepdims=True))
    centered = rows - mean
    spread = lax.optimization_barrier(jnp.mean(centered * centered, axis=-1, keepdims=True))
    return centered * lax.rsqrt(spread + EPS) * gain

def softmax_rows(scores):
    top = lax.optimization_barrier(jnp.max(scores, axis=-1, keepdims=True))
    expo = jnp.exp(scores - top)
    return expo / lax.optimization_barrier(jnp.sum(expo, axis=-1, keepdims=True))

def spatial_tile(frames_in, gain_one, spatial_qkv, spatial_out, gain_two, mlp_up, mlp_down):
    scale = 1.0 / math.sqrt(HD)
    normed = normalize(frames_in.astype(jnp.float32), gain_one).astype(jnp.bfloat16)
    qkv = jnp.einsum('spd,idc->spic', normed.astype(jnp.float32), spatial_qkv.astype(jnp.float32)).astype(jnp.bfloat16)
    query = qkv[:, :, 0].reshape(FRAMES, P_SIZE, HEADS, HD).astype(jnp.float32)
    key_all = qkv[:, :, 1].reshape(FRAMES, P_SIZE, HEADS, HD).astype(jnp.float32)
    value = qkv[:, :, 2].reshape(FRAMES, P_SIZE, HEADS, HD).astype(jnp.float32)
    scores = jnp.einsum('sqhe,skhe->shqk', query, key_all) * scale
    probs = softmax_rows(scores).astype(jnp.bfloat16)
    mixed = jnp.einsum('shqk,skhe->sqhe', probs.astype(jnp.float32), value).astype(jnp.bfloat16)
    mixed = mixed.reshape(FRAMES * P_SIZE, D)
    resid = frames_in.astype(jnp.float32).reshape(FRAMES * P_SIZE, D) + jnp.dot(mixed, spatial_out, preferred_element_type=jnp.float32)
    normed_two = normalize(resid, gain_two).astype(jnp.bfloat16)
    hidden = jax.nn.gelu(jnp.dot(normed_two, mlp_up, preferred_element_type=jnp.float32), approximate=False).astype(jnp.bfloat16)
    spatial = resid + jnp.dot(hidden, mlp_down, preferred_element_type=jnp.float32)
    return spatial.astype(jnp.bfloat16).reshape(FRAMES, P_SIZE, D)

def temporal_tile(spatial, counts, gain_three, temporal_qkv, temporal_out):
    scale = 1.0 / math.sqrt(HD)
    normed = normalize(spatial.astype(jnp.float32), gain_three).astype(jnp.bfloat16)
    qkv = jnp.einsum('fpd,idc->fpic', normed.astype(jnp.float32), temporal_qkv.astype(jnp.float32)).astype(jnp.bfloat16)
    query = qkv[:, :, 0].reshape(FRAMES, P_SIZE, HEADS, HD).astype(jnp.float32)
    key_all = qkv[:, :, 1].reshape(FRAMES, P_SIZE, HEADS, HD).astype(jnp.float32)
    value = qkv[:, :, 2].reshape(FRAMES, P_SIZE, HEADS, HD).astype(jnp.float32)
    bias = jnp.log((counts.astype(jnp.float32) + 1.0) / (PIX + 1.0))
    scores = jnp.einsum('fphe,gphe->phfg', query, key_all) * scale + jnp.transpose(bias)[:, None, None, :]
    probs = softmax_rows(scores).astype(jnp.bfloat16)
    mixed = jnp.einsum('phfg,gphe->fphe', probs.astype(jnp.float32), value).astype(jnp.bfloat16)
    mixed = mixed.reshape(FRAMES * P_SIZE, D)
    out = spatial.astype(jnp.float32).reshape(FRAMES * P_SIZE, D) + jnp.dot(mixed, temporal_out, preferred_element_type=jnp.float32)
    return out.astype(jnp.bfloat16).reshape(FRAMES, P_SIZE, D)

def reference(tokens, clear_count, gain_one, spatial_qkv, spatial_out, gain_two, mlp_up, mlp_down, gain_three, temporal_qkv, temporal_out):
    tiles = tokens.reshape(TILES, FRAMES, P_SIZE, D)
    counts = clear_count.reshape(TILES, FRAMES, P_SIZE)

    def one_tile(pair):
        frames_in, tile_counts = pair
        spatial = spatial_tile(frames_in, gain_one, spatial_qkv, spatial_out, gain_two, mlp_up, mlp_down)
        return temporal_tile(spatial, tile_counts, gain_three, temporal_qkv, temporal_out)
    result = lax.map(one_tile, (tiles, counts))
    return result.reshape(S, GROUPS, PQ, D)
```

```python
import math

import jax
import jax.numpy as jnp
from jax import lax
from jax.experimental import pallas as pl
from jax.experimental.pallas import tpu as pltpu
from jax.sharding import PartitionSpec as P

HD = 64
PIX = 256
FRAMES = 12
EPS = 1e-06
F = 3
N = 256
B = 64
D = 1024
C = 256
S = 96
DP = 32
BF = jnp.bfloat16
F32 = jnp.float32


def normalize(rows, gain):
    mean = jnp.sum(rows, axis=-1, keepdims=True) * (1.0 / D)
    centered = rows - mean
    spread = jnp.sum(centered * centered, axis=-1, keepdims=True) * (1.0 / D)
    return centered * lax.rsqrt(spread + EPS) * gain


def gelu(x):
    return 0.5 * x * (1.0 + lax.erf(x * (1.0 / math.sqrt(2.0))))


def at(start, size):
    return pl.ds(pl.multiple_of(start, size), size)


def dot(a, b):
    return jnp.dot(a, b, preferred_element_type=F32)


def dot_t(a, b):
    return lax.dot_general(a, b, (((1,), (1,)), ((), ())), preferred_element_type=F32)


def head_masks():
    lane = lax.broadcasted_iota(jnp.int32, (1, C), 1)
    return [(lane // HD == h) for h in range(C // HD)]


def kernel(
    tokens,
    counts,
    gain_one,
    gain_two,
    gain_three,
    w_qkv,
    w_out,
    w_up,
    w_down,
    t_qkv,
    t_out,
    out,
    tok,
    mix,
    qkv_v,
    out_v,
    up_v,
    down_v,
    tqkv_v,
    tout_v,
    normed,
    hidden,
    res,
    part,
    own,
    rs_send,
    rs_recv,
    rx_send,
    rx_recv,
    cells,
    a_send,
    a_recv,
    c_send,
    c_recv,
    tcells,
    xs,
    n3,
    q2,
    m2,
    loc,
    tok_s,
    tok_r,
    mix_s,
    mix_r,
    rs_s,
    rs_r,
    a_s,
    a_r,
    w_s,
    w_r,
):
    dp = lax.axis_index("dp")
    mp = lax.axis_index("mp")
    core = mp % 2
    sib_i = mp + 1 - 2 * core
    opp_i = (mp + 2) % 4
    diag_i = (sib_i + 2) % 4
    sib = {"mp": sib_i}
    opp = {"mp": opp_i}
    cell = (dp // 8) * 4 + dp % 4
    x_lo = (dp // 4) % 2

    def remote(src, dst, ss, rs, where):
        return pltpu.make_async_remote_copy(
            src_ref=src, dst_ref=dst, send_sem=ss, recv_sem=rs, device_id=where
        )

    def local_copy(src, dst, i):
        return pltpu.make_async_copy(src, dst, loc.at[i])

    loads = [
        local_copy(tokens, tok.at[:, at(mp * B, B)], 0),
        local_copy(w_qkv, qkv_v, 1),
        local_copy(w_out, out_v.at[at(mp * C, C)], 2),
        local_copy(w_up, up_v, 3),
        local_copy(w_down, down_v, 4),
        local_copy(t_qkv, tqkv_v, 5),
        local_copy(t_out, tout_v, 6),
    ]
    loads[0].start()
    loads[1].start()

    barrier = pltpu.get_barrier_semaphore()
    for i in range(1, 4):
        pl.semaphore_signal(barrier, inc=1, device_id={"mp": (mp + i) % 4})

    @pl.loop(1, DP)
    def _(i):
        pl.semaphore_signal(barrier, inc=1, device_id={"dp": (dp + i) % DP})

    row = lax.broadcasted_iota(jnp.int32, (8, 128), 0)
    lane = lax.broadcasted_iota(jnp.int32, (8, 128), 1)

    @pl.loop(0, DP)
    def _(d):
        tile = jnp.zeros((8, 128), jnp.int32)
        for f in range(F):
            for p in range(2):
                spot = (row == p) & (lane == dp * F + f)
                tile = jnp.where(spot, counts[f, d * 2 + p], tile)
        c_send[d] = tile.astype(F32)

    pl.semaphore_wait(barrier, DP + 2)

    first = remote(
        w_out.at[at(cell * 16, 16)],
        out_v.at[at(mp * C + cell * 16, 16)],
        w_s.at[0],
        w_r.at[0],
        opp,
    )
    first.start()

    def tok_copy(f, kind):
        blk = at(mp * B, B) if kind < 2 else at(opp_i * B, B)
        src = tokens.at[f] if kind < 2 else tok.at[f, blk]
        return remote(
            src, tok.at[f, blk], tok_s.at[kind, f], tok_r.at[kind, f], opp if kind == 0 else sib
        )

    for f in range(F):
        tok_copy(f, 0).start()
    for f in range(F):
        tok_copy(f, 1).start()
    own_w = remote(w_out, out_v.at[at(mp * C, C)], w_s.at[1], w_r.at[1], sib)
    own_w.start()
    for c in loads[2:]:
        c.start()

    c_send_own = c_send[dp]
    c_recv[dp] = c_send_own

    @pl.loop(1, DP)
    def _(i):
        to = (dp + i) % DP
        remote(c_send.at[to], c_recv.at[dp], a_s.at[F], a_r.at[F], {"dp": to}).start()

    first.wait_recv()
    mine = at(opp_i * C + cell * 16, 16)

    @pl.loop(1, 16)
    def _(j):
        q = (cell + j) % 16
        to = ((q // 4) * 2 + x_lo) * 4 + q % 4
        remote(out_v.at[mine], out_v.at[mine], w_s.at[2], w_r.at[2], {"dp": to}).start()

    masks = head_masks()

    def mix_copy(f, kind):
        cols = at(mp * C, C) if kind < 2 else at(opp_i * C, C)
        blk = mix.at[f, :, cols]
        return remote(
            blk, blk, mix_s.at[kind, f], mix_r.at[kind, f], opp if kind == 0 else sib
        )

    loads[0].wait()
    loads[1].wait()

    @pl.loop(0, F)
    def _(f):
        tok_copy(f, 0).wait_recv()
        tok_copy(f, 2).start()
        tok_copy(f, 1).wait_recv()
        tok_copy(f, 2).wait_recv()

        @pl.loop(0, N // 32)
        def _(i):
            rows = at(i * 32, 32)
            normed[rows] = normalize(tok[f, rows].astype(F32), gain_one[...]).astype(BF)

        q = dot(normed[...], qkv_v[0]) * (1.0 / math.sqrt(HD))
        k = dot(normed[...], qkv_v[1]).astype(BF)
        v = dot(normed[...], qkv_v[2]).astype(BF)
        total = None
        for h in range(C // HD):
            scores = dot_t(jnp.where(masks[h], q, 0.0).astype(BF), k)
            top = jnp.max(scores, axis=-1, keepdims=True)
            expo = jnp.exp(scores - top)
            denom = jnp.sum(expo, axis=-1, keepdims=True)
            mixed = dot(expo.astype(BF), v) / denom
            total = mixed if h == 0 else jnp.where(masks[h], mixed, total)
        mix[f, :, at(mp * C, C)] = total.astype(BF)
        mix_copy(f, 0).start()
        mix_copy(f, 1).start()

    fifteen = out_v.at[pl.ds(0, 240)]
    remote(fifteen, fifteen, w_s.at[2], w_r.at[2], sib).wait_recv()
    other = out_v.at[at(opp_i * C, C)]
    pass_w = remote(other, other, w_s.at[3], w_r.at[3], sib)
    pass_w.start()
    own_w.wait_recv()
    loads[2].wait()
    loads[3].wait()
    loads[4].wait()
    pass_w.wait_recv()

    def rs_copy(f):
        return remote(rs_send.at[f], rs_recv.at[f], rs_s.at[0, f], rs_r.at[0, f], sib)

    def rx_copy(f):
        return remote(rx_send.at[f], rx_recv.at[f], rs_s.at[1, f], rs_r.at[1, f], opp)

    def finish(f):
        rx_copy(f).wait_recv()
        value = own[f] + rx_recv[f].astype(F32)
        for c in range(8):
            cells[pl.ds(c, B, stride=8), :] = value[:, c * 128 : (c + 1) * 128]
        a_send[f] = cells[...].astype(BF).reshape(DP, 16, 128)
        a_recv[dp, f] = a_send[f, dp]

        @pl.loop(1, DP)
        def _(i):
            to = (dp + i) % DP
            remote(
                a_send.at[f, to], a_recv.at[dp, f], a_s.at[f], a_r.at[f], {"dp": to}
            ).start()

    @pl.loop(0, F)
    def _(f):
        mix_copy(f, 0).wait_recv()
        mix_copy(f, 2).start()
        mix_copy(f, 1).wait_recv()
        mix_copy(f, 2).wait_recv()
        for n in range(D // C):
            cols = pl.ds(n * C, C)
            res[:, cols] = dot(mix[f], out_v[:, cols]) + tok[f, :, cols].astype(F32)

        @pl.loop(0, N // 32)
        def _(i):
            rows = at(i * 32, 32)
            normed[rows] = normalize(res[rows], gain_two[...]).astype(BF)

        for n in range(D // C):
            cols = pl.ds(n * C, C)
            hidden[:, cols] = gelu(dot(normed[...], up_v[:, cols])).astype(BF)
        for n in range(D // C):
            cols = pl.ds(n * C, C)
            part[:, cols] = dot(hidden[...], down_v[:, cols])
        rs_send[f, 0] = part[at(sib_i * B, B)].astype(BF)
        rs_send[f, 1] = part[at(diag_i * B, B)].astype(BF)
        rs_copy(f).start()

        @pl.when(f > 0)
        def _():
            finish(f - 1)

        rs_copy(f).wait_recv()
        rx_send[f] = (part[at(opp_i * B, B)] + rs_recv[f, 1].astype(F32)).astype(BF)
        rx_copy(f).start()
        mine = at(mp * B, B)
        own[f] = res[mine] + part[mine] + rs_recv[f, 0].astype(F32)

    finish(F - 1)

    first.wait_send()
    own_w.wait_send()
    pass_w.wait_send()
    remote(fifteen, fifteen, w_s.at[2], w_r.at[2], sib).wait_send()
    for f in range(F):
        for kind in range(3):
            tok_copy(f, kind).wait_send()
            mix_copy(f, kind).wait_send()
        rs_copy(f).wait_send()
        rx_copy(f).wait_send()

    loads[5].wait()
    loads[6].wait()
    most = c_send.at[pl.ds(0, DP - 1)]
    count_done = remote(most, most, a_s.at[F], a_r.at[F], opp)
    count_done.wait_send()
    count_done.wait_recv()
    seen = c_recv[0]
    for i in range(1, DP):
        seen = seen + c_recv[i]
    bias = jnp.log((seen + 1.0) / (PIX + 1.0))
    block = a_send.at[0, pl.ds(0, DP - 1)]
    for f in range(F):
        done = remote(block, block, a_s.at[f], a_r.at[f], opp)
        done.wait_send()
        done.wait_recv()

    for i in range(8):
        tcells[pl.ds(i * 192, 192)] = a_recv[pl.ds(i * 4, 4)].reshape(192, 128).astype(F32)
    for p in range(2):
        for c in range(8):
            xs[pl.ds(p * S, S), pl.ds(c * 128, 128)] = tcells[
                pl.ds(p * 8 + c, S, stride=16), :
            ]

    @pl.loop(0, 2 * S // 32)
    def _(i):
        rows = at(i * 32, 32)
        n3[rows] = normalize(xs[rows], gain_three[...]).astype(BF)

    for i in range(3):
        for n in range(D // C):
            cols = pl.ds(n * C, C)
            q2[i, :, cols] = dot(n3[...], tqkv_v[i, :, cols]).astype(BF)

    one = lax.broadcasted_iota(jnp.int32, (S, S), 0) // FRAMES
    two = lax.broadcasted_iota(jnp.int32, (S, S), 1) // FRAMES
    same = one == two
    for p in range(2):
        rows = pl.ds(p * S, S)
        shift = jnp.where(same, bias[p : p + 1, :S], -1e30)
        for n in range(D // C):
            cols = pl.ds(n * C, C)
            q = q2[0, rows, cols].astype(F32) * (1.0 / math.sqrt(HD))
            k = q2[1, rows, cols]
            v = q2[2, rows, cols]
            total = None
            for h in range(C // HD):
                scores = dot_t(jnp.where(masks[h], q, 0.0).astype(BF), k) + shift
                top = jnp.max(scores, axis=-1, keepdims=True)
                expo = jnp.exp(scores - top)
                denom = jnp.sum(expo, axis=-1, keepdims=True)
                mixed = dot(expo.astype(BF), v) / denom
                total = mixed if h == 0 else jnp.where(masks[h], mixed, total)
            m2[rows, cols] = total.astype(BF)
    for n in range(D // C):
        cols = pl.ds(n * C, C)
        value = (xs[:, cols] + dot(m2[...], tout_v[:, cols])).astype(BF)
        out[:, :, cols] = value.reshape(2, S, C)


def local(
    tokens,
    clear_count,
    gain_one,
    spatial_qkv,
    spatial_out,
    gain_two,
    mlp_up,
    mlp_down,
    gain_three,
    temporal_qkv,
    temporal_out,
):
    hbm = pl.BlockSpec(memory_space=pl.ANY)
    vmem = pl.BlockSpec(memory_space=pltpu.VMEM)
    smem = pl.BlockSpec(memory_space=pltpu.SMEM)
    dma = pltpu.SemaphoreType.DMA
    scratch = [
        pltpu.VMEM((F, N, D), BF),
        pltpu.VMEM((F, N, D), BF),
        pltpu.VMEM((3, D, C), BF),
        pltpu.VMEM((D, D), BF),
        pltpu.VMEM((D, D), BF),
        pltpu.VMEM((D, D), BF),
        pltpu.VMEM((3, D, D), BF),
        pltpu.VMEM((D, D), BF),
        pltpu.VMEM((N, D), BF),
        pltpu.VMEM((N, D), BF),
        pltpu.VMEM((N, D), F32),
        pltpu.VMEM((N, D), F32),
        pltpu.VMEM((F, B, D), F32),
        pltpu.VMEM((F, 2, B, D), BF),
        pltpu.VMEM((F, 2, B, D), BF),
        pltpu.VMEM((F, B, D), BF),
        pltpu.VMEM((F, B, D), BF),
        pltpu.VMEM((B * 8, 128), F32),
        pltpu.VMEM((F, DP, 16, 128), BF),
        pltpu.VMEM((DP, F, 16, 128), BF),
        pltpu.VMEM((DP, 8, 128), F32),
        pltpu.VMEM((DP, 8, 128), F32),
        pltpu.VMEM((S * 16, 128), F32),
        pltpu.VMEM((2 * S, D), F32),
        pltpu.VMEM((2 * S, D), BF),
        pltpu.VMEM((3, 2 * S, D), BF),
        pltpu.VMEM((2 * S, D), BF),
        dma((7,)),
        dma((3, F)),
        dma((3, F)),
        dma((3, F)),
        dma((3, F)),
        dma((2, F)),
        dma((2, F)),
        dma((F + 1,)),
        dma((F + 1,)),
        dma((4,)),
        dma((4,)),
    ]
    rows = pl.pallas_call(
        kernel,
        out_shape=jax.ShapeDtypeStruct((2, S, D), BF),
        in_specs=[hbm, smem, vmem, vmem, vmem, hbm, hbm, hbm, hbm, hbm, hbm],
        out_specs=vmem,
        scratch_shapes=scratch,
        compiler_params=pltpu.CompilerParams(
            collective_id=0, has_side_effects=True, vmem_limit_bytes=60 * 1024 * 1024
        ),
        name="layers",
    )(
        tokens,
        clear_count,
        gain_one.reshape(1, D),
        gain_two.reshape(1, D),
        gain_three.reshape(1, D),
        spatial_qkv,
        spatial_out,
        mlp_up,
        mlp_down,
        temporal_qkv,
        temporal_out,
    )
    return jnp.transpose(rows, (1, 0, 2)).reshape(S, 1, 2, D)


def solution(mesh):
    placed = (
        P("dp", "mp", None),
        P("dp", "mp"),
        P(),
        P(None, None, "mp"),
        P("mp", None),
        P(),
        P(None, "mp"),
        P("mp", None),
        P(),
        P(),
        P(),
    )
    return jax.shard_map(
        local, mesh=mesh, in_specs=placed, out_specs=P(None, "mp", "dp", None), check_vma=False
    )
```

```python
import math

import jax
import jax.numpy as jnp
from jax import lax
from jax.experimental import pallas as pl
from jax.experimental.pallas import tpu as pltpu
from jax.sharding import PartitionSpec as P

HD = 64
PIX = 256
FRAMES = 12
EPS = 1e-06
F = 3
N = 256
H = 128
B = 64
D = 1024
C = 256
S = 96
DP = 32
BF = jnp.bfloat16
F32 = jnp.float32


def normalize(rows, gain):
    mean = jnp.sum(rows, axis=-1, keepdims=True) * (1.0 / D)
    centered = rows - mean
    spread = jnp.sum(centered * centered, axis=-1, keepdims=True) * (1.0 / D)
    return centered * lax.rsqrt(spread + EPS) * gain


def gelu(x):
    return 0.5 * x * (1.0 + lax.erf(x * (1.0 / math.sqrt(2.0))))


def at(start, size):
    return pl.ds(pl.multiple_of(start, size), size)


def dot(a, b):
    return jnp.dot(a, b, preferred_element_type=F32)


def dot_t(a, b):
    return lax.dot_general(a, b, (((1,), (1,)), ((), ())), preferred_element_type=F32)


def head_masks():
    lane = lax.broadcasted_iota(jnp.int32, (1, C), 1)
    return [(lane // HD == h) for h in range(C // HD)]


def attend(q, k, v, masks, shift):
    total = None
    for h in range(C // HD):
        scores = dot_t(jnp.where(masks[h], q, 0.0).astype(BF), k)
        if shift is not None:
            scores = scores + shift
        top = jnp.max(scores, axis=-1, keepdims=True)
        expo = jnp.exp(scores - top)
        denom = jnp.sum(expo, axis=-1, keepdims=True)
        mixed = dot(expo.astype(BF), v) * (1.0 / denom)
        total = mixed if h == 0 else jnp.where(masks[h], mixed, total)
    return total.astype(BF)


def kernel(
    tokens,
    counts,
    gain_one,
    gain_two,
    gain_three,
    w_qkv,
    w_out,
    w_up,
    w_down,
    t_qkv,
    t_out,
    out,
    tok,
    heads,
    mix,
    qkv_v,
    out_v,
    up_v,
    down_v,
    tqkv_v,
    tout_v,
    normed,
    hidden,
    res,
    part,
    own,
    rx_send,
    rx_recv,
    cells,
    a_send,
    a_recv,
    c_send,
    c_recv,
    tcells,
    xs,
    n3,
    q2,
    m2,
    loc,
    tok_s,
    tok_r,
    mix_s,
    mix_r,
    rx_s,
    rx_r,
    a_s,
    a_r,
    w_s,
    w_r,
):
    dp = lax.axis_index("dp")
    mp = lax.axis_index("mp")
    core = mp % 2
    x_hi = mp // 2
    opp_i = (mp + 2) % 4
    sib = {"mp": mp + 1 - 2 * core}
    opp = {"mp": opp_i}
    diag = {"mp": (mp + 3 - 2 * core) % 4}
    cell = (dp // 8) * 4 + dp % 4
    x_lo = (dp // 4) % 2
    half = at(core * H, H)
    other = at((1 - core) * H, H)
    own_rows = at(core * H + x_hi * B, B)
    opp_rows = at(core * H + (1 - x_hi) * B, B)
    in_half = at(x_hi * B, B)
    in_half_opp = at((1 - x_hi) * B, B)

    def remote(src, dst, ss, rs, where):
        return pltpu.make_async_remote_copy(
            src_ref=src, dst_ref=dst, send_sem=ss, recv_sem=rs, device_id=where
        )

    def local_copy(src, dst, i):
        return pltpu.make_async_copy(src, dst, loc.at[i])

    units = at(core * D, D)
    loads = [
        local_copy(tokens, tok.at[:, own_rows], 0),
        local_copy(w_qkv, qkv_v, 1),
        local_copy(w_out, out_v.at[at(mp * C, C)], 2),
        local_copy(w_up, up_v.at[core], 3),
        local_copy(w_down, down_v.at[units], 4),
        local_copy(t_qkv, tqkv_v, 5),
        local_copy(t_out, tout_v, 6),
    ]

    barrier = pltpu.get_barrier_semaphore()
    for i in range(1, 4):
        pl.semaphore_signal(barrier, inc=1, device_id={"mp": (mp + i) % 4})

    @pl.loop(1, DP)
    def _(i):
        pl.semaphore_signal(barrier, inc=1, device_id={"dp": (dp + i) % DP})

    loads[0].start()
    loads[1].start()
    pl.semaphore_wait(barrier, DP + 2)

    first = remote(
        w_out.at[at(cell * 16, 16)],
        out_v.at[at(mp * C + cell * 16, 16)],
        w_s.at[0],
        w_r.at[0],
        opp,
    )
    first.start()

    def tok_copy(f, kind):
        if kind < 2:
            return remote(
                tokens.at[f],
                tok.at[f, own_rows],
                tok_s.at[kind, f],
                tok_r.at[kind, f],
                opp if kind == 0 else sib,
            )
        blk = tok.at[f, opp_rows]
        return remote(blk, blk, tok_s.at[kind, f], tok_r.at[kind, f], sib)

    for f in range(F):
        tok_copy(f, 0).start()
    for f in range(F):
        tok_copy(f, 1).start()
    for c in loads[2:5]:
        c.start()
    to_sib = [
        remote(w_out, out_v.at[at(mp * C, C)], w_s.at[1], w_r.at[1], sib),
        remote(w_up, up_v.at[core], w_s.at[4], w_r.at[4], sib),
        remote(w_down, down_v.at[units], w_s.at[5], w_r.at[5], sib),
    ]
    for c in to_sib:
        c.start()

    row = lax.broadcasted_iota(jnp.int32, (8, 128), 0)
    lane = lax.broadcasted_iota(jnp.int32, (8, 128), 1)

    @pl.loop(0, DP)
    def _(d):
        tile = jnp.zeros((8, 128), jnp.int32)
        for f in range(F):
            for p in range(2):
                spot = (row == p) & (lane == f * DP + dp)
                tile = jnp.where(spot, counts[f, d * 2 + p], tile)
        c_send[d] = tile.astype(F32)

    c_recv[dp] = c_send[dp]

    first.wait_recv()
    mine = at(opp_i * C + cell * 16, 16)

    @pl.loop(1, 16)
    def _(j):
        q = (cell + j) % 16
        to = ((q // 4) * 2 + x_lo) * 4 + q % 4
        remote(out_v.at[mine], out_v.at[mine], w_s.at[2], w_r.at[2], {"dp": to}).start()

    @pl.loop(1, DP)
    def _(i):
        to = (dp + i) % DP
        remote(c_send.at[to], c_recv.at[dp], a_s.at[F], a_r.at[F], {"dp": to}).start()

    masks = head_masks()
    cols_mp = at(mp * C, C)

    def mix_copy(f, kind):
        src = heads.at[f, half if kind == 0 else other]
        dst = mix.at[f, :, cols_mp]
        return remote(
            src, dst, mix_s.at[kind, f], mix_r.at[kind, f], (opp, diag, sib)[kind]
        )

    loads[0].wait()
    loads[1].wait()

    @pl.loop(0, F + 1)
    def _(step):
        @pl.when(step < F)
        def _():
            tok_copy(step, 0).wait_recv()
            tok_copy(step, 2).start()

        @pl.when(step > 0)
        def _():
            f = step - 1
            tok_copy(f, 1).wait_recv()
            tok_copy(f, 2).wait_recv()
            normed[...] = normalize(tok[f].astype(F32), gain_one[...]).astype(BF)
            q = dot(normed[...], qkv_v[0]) * (1.0 / math.sqrt(HD))
            k = dot(normed[...], qkv_v[1]).astype(BF)
            v = dot(normed[...], qkv_v[2]).astype(BF)
            heads[f] = attend(q, k, v, masks, None)
            for kind in range(3):
                mix_copy(f, kind).start()
            mix[f, :, cols_mp] = heads[f, half]

    fifteen = out_v.at[pl.ds(0, 240)]
    remote(fifteen, fifteen, w_s.at[2], w_r.at[2], sib).wait_recv()
    block = out_v.at[at(opp_i * C, C)]
    pass_w = remote(block, block, w_s.at[3], w_r.at[3], sib)
    pass_w.start()
    for c in loads[5:]:
        c.start()
    for c in loads[2:5]:
        c.wait()
    for c in to_sib:
        c.wait_recv()
    pass_w.wait_recv()

    def rx_copy(f):
        return remote(rx_send.at[f], rx_recv.at[f], rx_s.at[f], rx_r.at[f], opp)

    @pl.loop(0, F)
    def _(f):
        for kind in range(3):
            mix_copy(f, kind).wait_recv()
        res[...] = dot(mix[f], out_v[...]) + tok[f, half].astype(F32)
        normed[:H] = normalize(res[...], gain_two[...]).astype(BF)
        for j in range(2):
            for n in range(D // C):
                cols = pl.ds(n * C, C)
                hidden[:, pl.ds(j * D + n * C, C)] = gelu(
                    dot(normed[:H], up_v[j, :, cols])
                ).astype(BF)
        part[...] = dot(hidden[...], down_v[...])
        rx_send[f] = part[in_half_opp].astype(BF)
        rx_copy(f).start()
        own[f] = res[in_half] + part[in_half]

    def parcels(f):
        rx_copy(f).wait_recv()
        value = own[f] + rx_recv[f].astype(F32)
        for c in range(8):
            cells[pl.ds(c, B, stride=8), :] = value[:, c * 128 : (c + 1) * 128]
        a_send[f] = cells[...].astype(BF).reshape(DP, 16, 128)
        a_recv[f, dp] = a_send[f, dp]

        @pl.loop(1, DP)
        def _(i):
            to = (dp + i) % DP
            remote(
                a_send.at[f, to], a_recv.at[f, dp], a_s.at[f], a_r.at[f], {"dp": to}
            ).start()

    for f in range(F):
        parcels(f)

    first.wait_send()
    for c in to_sib:
        c.wait_send()
    pass_w.wait_send()
    remote(fifteen, fifteen, w_s.at[2], w_r.at[2], sib).wait_send()
    for f in range(F):
        for kind in range(3):
            tok_copy(f, kind).wait_send()
            mix_copy(f, kind).wait_send()
        rx_copy(f).wait_send()

    loads[5].wait()
    loads[6].wait()
    most = c_send.at[pl.ds(0, DP - 1)]
    count_done = remote(most, most, a_s.at[F], a_r.at[F], opp)
    count_done.wait_send()
    count_done.wait_recv()
    seen = c_recv[0]
    for i in range(1, DP):
        seen = seen + c_recv[i]
    bias = jnp.log((seen + 1.0) / (PIX + 1.0))
    group = lax.broadcasted_iota(jnp.int32, (S, S), 0) % DP // (FRAMES // F)
    key_group = lax.broadcasted_iota(jnp.int32, (S, S), 1) % DP // (FRAMES // F)
    same = group == key_group

    def arrive(f):
        block = a_send.at[f, pl.ds(0, DP - 1)]
        done = remote(block, block, a_s.at[f], a_r.at[f], opp)
        done.wait_send()
        done.wait_recv()
        tcells[...] = a_recv[f].reshape(DP * 16, 128).astype(F32)
        for p in range(2):
            for c in range(8):
                xs[pl.ds(p * S + f * DP, DP), pl.ds(c * 128, 128)] = tcells[
                    pl.ds(p * 8 + c, DP, stride=16), :
                ]
            n3[pl.ds(f * 2 * DP + p * DP, DP)] = normalize(
                xs[pl.ds(p * S + f * DP, DP)], gain_three[...]
            ).astype(BF)

    def project(frames):
        rows = n3[pl.ds(frames[0] * 2 * DP, len(frames) * 2 * DP)]
        for i in range(3):
            for n in range(D // C):
                cols = pl.ds(n * C, C)
                value = dot(rows, tqkv_v[i, :, cols])
                if i == 0:
                    value = value * (1.0 / math.sqrt(HD))
                value = value.astype(BF)
                for j, f in enumerate(frames):
                    for p in range(2):
                        start = (j * 2 + p) * DP
                        q2[i, pl.ds(p * S + f * DP, DP), cols] = value[start : start + DP]

    arrive(0)
    arrive(1)
    project((0, 1))
    arrive(2)
    project((2,))

    for p in range(2):
        rows = pl.ds(p * S, S)
        shift = jnp.where(same, bias[p : p + 1, :S], -1e30)
        for n in range(D // C):
            cols = pl.ds(n * C, C)
            q = q2[0, rows, cols].astype(F32)
            m2[rows, cols] = attend(q, q2[1, rows, cols], q2[2, rows, cols], masks, shift)
    value = (xs[...] + dot(m2[...], tout_v[...])).astype(BF)
    out[...] = value.reshape(2, S, D)


def local(
    tokens,
    clear_count,
    gain_one,
    spatial_qkv,
    spatial_out,
    gain_two,
    mlp_up,
    mlp_down,
    gain_three,
    temporal_qkv,
    temporal_out,
):
    hbm = pl.BlockSpec(memory_space=pl.ANY)
    vmem = pl.BlockSpec(memory_space=pltpu.VMEM)
    smem = pl.BlockSpec(memory_space=pltpu.SMEM)
    dma = pltpu.SemaphoreType.DMA
    scratch = [
        pltpu.VMEM((F, N, D), BF),
        pltpu.VMEM((F, N, C), BF),
        pltpu.VMEM((F, H, D), BF),
        pltpu.VMEM((3, D, C), BF),
        pltpu.VMEM((D, D), BF),
        pltpu.VMEM((2, D, D), BF),
        pltpu.VMEM((2 * D, D), BF),
        pltpu.VMEM((3, D, D), BF),
        pltpu.VMEM((D, D), BF),
        pltpu.VMEM((N, D), BF),
        pltpu.VMEM((H, 2 * D), BF),
        pltpu.VMEM((H, D), F32),
        pltpu.VMEM((H, D), F32),
        pltpu.VMEM((F, B, D), F32),
        pltpu.VMEM((F, B, D), BF),
        pltpu.VMEM((F, B, D), BF),
        pltpu.VMEM((B * 8, 128), F32),
        pltpu.VMEM((F, DP, 16, 128), BF),
        pltpu.VMEM((F, DP, 16, 128), BF),
        pltpu.VMEM((DP, 8, 128), F32),
        pltpu.VMEM((DP, 8, 128), F32),
        pltpu.VMEM((DP * 16, 128), F32),
        pltpu.VMEM((2 * S, D), F32),
        pltpu.VMEM((2 * S, D), BF),
        pltpu.VMEM((3, 2 * S, D), BF),
        pltpu.VMEM((2 * S, D), BF),
        dma((7,)),
        dma((3, F)),
        dma((3, F)),
        dma((3, F)),
        dma((3, F)),
        dma((F,)),
        dma((F,)),
        dma((F + 1,)),
        dma((F + 1,)),
        dma((6,)),
        dma((6,)),
    ]
    rows = pl.pallas_call(
        kernel,
        out_shape=jax.ShapeDtypeStruct((2, S, D), BF),
        in_specs=[hbm, smem, vmem, vmem, vmem, hbm, hbm, hbm, hbm, hbm, hbm],
        out_specs=vmem,
        scratch_shapes=scratch,
        compiler_params=pltpu.CompilerParams(
            collective_id=0, has_side_effects=True, vmem_limit_bytes=60 * 1024 * 1024
        ),
        name="layers",
    )(
        tokens,
        clear_count,
        gain_one.reshape(1, D),
        gain_two.reshape(1, D),
        gain_three.reshape(1, D),
        spatial_qkv,
        spatial_out,
        mlp_up,
        mlp_down,
        temporal_qkv,
        temporal_out,
    )
    rows = rows.reshape(2, F, DP, D)
    return jnp.transpose(rows, (2, 1, 0, 3)).reshape(S, 1, 2, D)


def solution(mesh):
    placed = (
        P("dp", "mp", None),
        P("dp", "mp"),
        P(),
        P(None, None, "mp"),
        P("mp", None),
        P(),
        P(None, "mp"),
        P("mp", None),
        P(),
        P(),
        P(),
    )
    return jax.shard_map(
        local, mesh=mesh, in_specs=placed, out_specs=P(None, "mp", "dp", None), check_vma=False
    )
```

```python
import math

import jax
import jax.numpy as jnp
from jax import lax
from jax.experimental import pallas as pl
from jax.experimental.pallas import tpu as pltpu
from jax.sharding import PartitionSpec as P

HD = 64
PIX = 256
FRAMES = 12
EPS = 1e-06
F = 3
N = 256
H = 128
B = 64
D = 1024
C = 256
S = 96
DP = 32
BF = jnp.bfloat16
F32 = jnp.float32


def normalize(rows, gain):
    mean = jnp.sum(rows, axis=-1, keepdims=True) * (1.0 / D)
    centered = rows - mean
    spread = jnp.sum(centered * centered, axis=-1, keepdims=True) * (1.0 / D)
    return centered * lax.rsqrt(spread + EPS) * gain


def gelu(x):
    return 0.5 * x * (1.0 + lax.erf(x * (1.0 / math.sqrt(2.0))))


def at(start, size):
    return pl.ds(pl.multiple_of(start, size), size)


def dot(a, b):
    return jnp.dot(a, b, preferred_element_type=F32)


def dot_t(a, b):
    return lax.dot_general(a, b, (((1,), (1,)), ((), ())), preferred_element_type=F32)


def head_masks():
    lane = lax.broadcasted_iota(jnp.int32, (1, C), 1)
    return [(lane // HD == h) for h in range(C // HD)]


def attend(q, k, v, masks, shift):
    total = None
    for h in range(C // HD):
        scores = dot_t(jnp.where(masks[h], q, 0.0).astype(BF), k)
        if shift is not None:
            scores = scores + shift
        top = jnp.max(scores, axis=-1, keepdims=True)
        expo = jnp.exp(scores - top)
        denom = jnp.sum(expo, axis=-1, keepdims=True)
        mixed = dot(expo.astype(BF), v) * (1.0 / denom)
        total = mixed if h == 0 else jnp.where(masks[h], mixed, total)
    return total.astype(BF)


def kernel(
    tokens,
    counts,
    gain_one,
    gain_two,
    gain_three,
    w_qkv,
    w_out,
    w_up,
    w_down,
    t_qkv,
    t_out,
    out,
    tok,
    heads,
    mix,
    qkv_v,
    out_v,
    up_v,
    down_v,
    tqkv_v,
    tout_v,
    normed,
    hidden,
    res,
    part,
    own,
    rx_send,
    rx_recv,
    cells,
    a_send,
    a_recv,
    c_send,
    c_recv,
    tcells,
    xs,
    n3,
    q2,
    m2,
    loc,
    tok_s,
    tok_r,
    mix_s,
    mix_r,
    rx_s,
    rx_r,
    a_s,
    a_r,
    w_s,
    w_r,
    rounds,
):
    dp = lax.axis_index("dp")
    mp = lax.axis_index("mp")
    core = mp % 2
    x_hi = mp // 2
    opp_i = (mp + 2) % 4
    sib = {"mp": mp + 1 - 2 * core}
    opp = {"mp": opp_i}
    diag = {"mp": (mp + 3 - 2 * core) % 4}
    cell = (dp // 8) * 4 + dp % 4
    x_lo = (dp // 4) % 2
    half = at(core * H, H)
    other = at((1 - core) * H, H)
    own_rows = at(core * H + x_hi * B, B)
    opp_rows = at(core * H + (1 - x_hi) * B, B)
    in_half = at(x_hi * B, B)
    in_half_opp = at((1 - x_hi) * B, B)

    def remote(src, dst, ss, rs, where):
        return pltpu.make_async_remote_copy(
            src_ref=src, dst_ref=dst, send_sem=ss, recv_sem=rs, device_id=where
        )

    def local_copy(src, dst, i):
        return pltpu.make_async_copy(src, dst, loc.at[i])

    units = at(core * D, D)
    loads = [
        local_copy(tokens, tok.at[:, own_rows], 0),
        local_copy(w_qkv, qkv_v, 1),
        local_copy(w_out, out_v.at[at(mp * C, C)], 2),
        local_copy(w_up, up_v.at[core], 3),
        local_copy(w_down, down_v.at[units], 4),
        local_copy(t_qkv, tqkv_v, 5),
        local_copy(t_out, tout_v, 6),
    ]

    barrier = pltpu.get_barrier_semaphore()
    for i in range(1, 4):
        pl.semaphore_signal(barrier, inc=1, device_id={"mp": (mp + i) % 4})

    y, z = dp // 8, dp % 4
    near = [{"dp": (((y + i) % 4) * 2 + x_lo) * 4 + z} for i in (1, 2, 3)]
    near += [{"dp": dp - z + (z + i) % 4} for i in (1, 2, 3)]
    near += [{"dp": (y * 2 + 1 - x_lo) * 4 + z}]
    for who in near:
        pl.semaphore_signal(barrier, inc=1, device_id=who)
    loads[0].start()
    loads[1].start()
    pl.semaphore_wait(barrier, 3 + len(near))

    first = remote(
        w_out.at[at(cell * 16, 16)],
        out_v.at[at(mp * C + cell * 16, 16)],
        w_s.at[0],
        w_r.at[0],
        opp,
    )
    first.start()

    def tok_copy(f, kind):
        if kind < 2:
            return remote(
                tokens.at[f],
                tok.at[f, own_rows],
                tok_s.at[kind, f],
                tok_r.at[kind, f],
                opp if kind == 0 else sib,
            )
        blk = tok.at[f, opp_rows]
        return remote(blk, blk, tok_s.at[kind, f], tok_r.at[kind, f], sib)

    for f in range(F):
        tok_copy(f, 0).start()
    for f in range(F):
        tok_copy(f, 1).start()
    for who in near:
        pl.semaphore_signal(rounds.at[0], inc=1, device_id=who)
    for c in loads[2:5]:
        c.start()
    to_sib = [
        remote(w_out, out_v.at[at(mp * C, C)], w_s.at[1], w_r.at[1], sib),
        remote(w_up, up_v.at[core], w_s.at[4], w_r.at[4], sib),
        remote(w_down, down_v.at[units], w_s.at[5], w_r.at[5], sib),
    ]
    for c in to_sib:
        c.start()

    row = lax.broadcasted_iota(jnp.int32, (8, 128), 0)
    lane = lax.broadcasted_iota(jnp.int32, (8, 128), 1)

    @pl.loop(0, DP)
    def _(d):
        tile = jnp.zeros((8, 128), jnp.int32)
        for f in range(F):
            for p in range(2):
                spot = (row == p) & (lane == f * DP + dp)
                tile = jnp.where(spot, counts[f, d * 2 + p], tile)
        c_send[d] = tile.astype(F32)

    c_recv[dp] = c_send[dp]

    pl.semaphore_wait(rounds.at[0], len(near))
    for who in near:
        pl.semaphore_signal(rounds.at[1], inc=1, device_id=who)
    first.wait_recv()
    mine = at(opp_i * C + cell * 16, 16)

    @pl.loop(1, 16)
    def _(j):
        q = (cell + j) % 16
        to = ((q // 4) * 2 + x_lo) * 4 + q % 4
        remote(out_v.at[mine], out_v.at[mine], w_s.at[2], w_r.at[2], {"dp": to}).start()

    pl.semaphore_wait(rounds.at[1], len(near))

    @pl.loop(1, DP)
    def _(i):
        to = (dp + i) % DP
        remote(c_send.at[to], c_recv.at[dp], a_s.at[F], a_r.at[F], {"dp": to}).start()

    masks = head_masks()
    cols_mp = at(mp * C, C)

    def mix_copy(f, kind):
        src = heads.at[f, half if kind == 0 else other]
        dst = mix.at[f, :, cols_mp]
        return remote(
            src, dst, mix_s.at[kind, f], mix_r.at[kind, f], (opp, diag, sib)[kind]
        )

    loads[0].wait()
    loads[1].wait()

    @pl.loop(0, F + 1)
    def _(step):
        @pl.when(step < F)
        def _():
            tok_copy(step, 0).wait_recv()
            tok_copy(step, 2).start()

        @pl.when(step > 0)
        def _():
            f = step - 1
            tok_copy(f, 1).wait_recv()
            tok_copy(f, 2).wait_recv()
            normed[...] = normalize(tok[f].astype(F32), gain_one[...]).astype(BF)
            q = dot(normed[...], qkv_v[0]) * (1.0 / math.sqrt(HD))
            k = dot(normed[...], qkv_v[1]).astype(BF)
            v = dot(normed[...], qkv_v[2]).astype(BF)
            heads[f] = attend(q, k, v, masks, None)
            for kind in range(3):
                mix_copy(f, kind).start()
            mix[f, :, cols_mp] = heads[f, half]

    fifteen = out_v.at[pl.ds(0, 240)]
    remote(fifteen, fifteen, w_s.at[2], w_r.at[2], sib).wait_recv()
    block = out_v.at[at(opp_i * C, C)]
    pass_w = remote(block, block, w_s.at[3], w_r.at[3], sib)
    pass_w.start()
    for c in loads[5:]:
        c.start()
    for c in loads[2:5]:
        c.wait()
    for c in to_sib:
        c.wait_recv()
    pass_w.wait_recv()

    def rx_copy(f):
        return remote(rx_send.at[f], rx_recv.at[f], rx_s.at[f], rx_r.at[f], opp)

    @pl.loop(0, F)
    def _(f):
        for kind in range(3):
            mix_copy(f, kind).wait_recv()
        res[...] = dot(mix[f], out_v[...]) + tok[f, half].astype(F32)
        normed[:H] = normalize(res[...], gain_two[...]).astype(BF)
        for j in range(2):
            for n in range(D // C):
                cols = pl.ds(n * C, C)
                hidden[:, pl.ds(j * D + n * C, C)] = gelu(
                    dot(normed[:H], up_v[j, :, cols])
                ).astype(BF)
        part[...] = dot(hidden[...], down_v[...])
        rx_send[f] = part[in_half_opp].astype(BF)
        rx_copy(f).start()
        own[f] = res[in_half] + part[in_half]

    def parcels(f):
        rx_copy(f).wait_recv()
        value = own[f] + rx_recv[f].astype(F32)
        for c in range(8):
            cells[pl.ds(c, B, stride=8), :] = value[:, c * 128 : (c + 1) * 128]
        a_send[f] = cells[...].astype(BF).reshape(DP, 16, 128)
        a_recv[f, dp] = a_send[f, dp]

        @pl.loop(1, DP)
        def _(i):
            to = (dp + i) % DP
            remote(
                a_send.at[f, to], a_recv.at[f, dp], a_s.at[f], a_r.at[f], {"dp": to}
            ).start()

    for f in range(F):
        parcels(f)

    first.wait_send()
    for c in to_sib:
        c.wait_send()
    pass_w.wait_send()
    remote(fifteen, fifteen, w_s.at[2], w_r.at[2], sib).wait_send()
    for f in range(F):
        for kind in range(3):
            tok_copy(f, kind).wait_send()
            mix_copy(f, kind).wait_send()
        rx_copy(f).wait_send()

    loads[5].wait()
    loads[6].wait()
    most = c_send.at[pl.ds(0, DP - 1)]
    count_done = remote(most, most, a_s.at[F], a_r.at[F], opp)
    count_done.wait_send()
    count_done.wait_recv()
    seen = c_recv[0]
    for i in range(1, DP):
        seen = seen + c_recv[i]
    bias = jnp.log((seen + 1.0) / (PIX + 1.0))
    group = lax.broadcasted_iota(jnp.int32, (S, S), 0) % DP // (FRAMES // F)
    key_group = lax.broadcasted_iota(jnp.int32, (S, S), 1) % DP // (FRAMES // F)
    same = group == key_group

    def arrive(f):
        block = a_send.at[f, pl.ds(0, DP - 1)]
        done = remote(block, block, a_s.at[f], a_r.at[f], opp)
        done.wait_send()
        done.wait_recv()
        tcells[...] = a_recv[f].reshape(DP * 16, 128).astype(F32)
        for p in range(2):
            for c in range(8):
                xs[pl.ds(p * S + f * DP, DP), pl.ds(c * 128, 128)] = tcells[
                    pl.ds(p * 8 + c, DP, stride=16), :
                ]
            n3[pl.ds(f * 2 * DP + p * DP, DP)] = normalize(
                xs[pl.ds(p * S + f * DP, DP)], gain_three[...]
            ).astype(BF)

    def project(frames):
        rows = n3[pl.ds(frames[0] * 2 * DP, len(frames) * 2 * DP)]
        for i in range(3):
            for n in range(D // C):
                cols = pl.ds(n * C, C)
                value = dot(rows, tqkv_v[i, :, cols])
                if i == 0:
                    value = value * (1.0 / math.sqrt(HD))
                value = value.astype(BF)
                for j, f in enumerate(frames):
                    for p in range(2):
                        start = (j * 2 + p) * DP
                        q2[i, pl.ds(p * S + f * DP, DP), cols] = value[start : start + DP]

    arrive(0)
    project((0,))
    arrive(1)
    arrive(2)
    project((1, 2))

    for p in range(2):
        rows = pl.ds(p * S, S)
        shift = jnp.where(same, bias[p : p + 1, :S], -1e30)
        for n in range(D // C):
            cols = pl.ds(n * C, C)
            q = q2[0, rows, cols].astype(F32)
            m2[rows, cols] = attend(q, q2[1, rows, cols], q2[2, rows, cols], masks, shift)
    value = (xs[...] + dot(m2[...], tout_v[...])).astype(BF)
    out[...] = value.reshape(2, S, D)


def local(
    tokens,
    clear_count,
    gain_one,
    spatial_qkv,
    spatial_out,
    gain_two,
    mlp_up,
    mlp_down,
    gain_three,
    temporal_qkv,
    temporal_out,
):
    hbm = pl.BlockSpec(memory_space=pl.ANY)
    vmem = pl.BlockSpec(memory_space=pltpu.VMEM)
    smem = pl.BlockSpec(memory_space=pltpu.SMEM)
    dma = pltpu.SemaphoreType.DMA
    scratch = [
        pltpu.VMEM((F, N, D), BF),
        pltpu.VMEM((F, N, C), BF),
        pltpu.VMEM((F, H, D), BF),
        pltpu.VMEM((3, D, C), BF),
        pltpu.VMEM((D, D), BF),
        pltpu.VMEM((2, D, D), BF),
        pltpu.VMEM((2 * D, D), BF),
        pltpu.VMEM((3, D, D), BF),
        pltpu.VMEM((D, D), BF),
        pltpu.VMEM((N, D), BF),
        pltpu.VMEM((H, 2 * D), BF),
        pltpu.VMEM((H, D), F32),
        pltpu.VMEM((H, D), F32),
        pltpu.VMEM((F, B, D), F32),
        pltpu.VMEM((F, B, D), BF),
        pltpu.VMEM((F, B, D), BF),
        pltpu.VMEM((B * 8, 128), F32),
        pltpu.VMEM((F, DP, 16, 128), BF),
        pltpu.VMEM((F, DP, 16, 128), BF),
        pltpu.VMEM((DP, 8, 128), F32),
        pltpu.VMEM((DP, 8, 128), F32),
        pltpu.VMEM((DP * 16, 128), F32),
        pltpu.VMEM((2 * S, D), F32),
        pltpu.VMEM((2 * S, D), BF),
        pltpu.VMEM((3, 2 * S, D), BF),
        pltpu.VMEM((2 * S, D), BF),
        dma((7,)),
        dma((3, F)),
        dma((3, F)),
        dma((3, F)),
        dma((3, F)),
        dma((F,)),
        dma((F,)),
        dma((F + 1,)),
        dma((F + 1,)),
        dma((6,)),
        dma((6,)),
        pltpu.SemaphoreType.REGULAR((2,)),
    ]
    rows = pl.pallas_call(
        kernel,
        out_shape=jax.ShapeDtypeStruct((2, S, D), BF),
        in_specs=[hbm, smem, vmem, vmem, vmem, hbm, hbm, hbm, hbm, hbm, hbm],
        out_specs=vmem,
        scratch_shapes=scratch,
        compiler_params=pltpu.CompilerParams(
            collective_id=0, has_side_effects=True, vmem_limit_bytes=60 * 1024 * 1024
        ),
        name="layers",
    )(
        tokens,
        clear_count,
        gain_one.reshape(1, D),
        gain_two.reshape(1, D),
        gain_three.reshape(1, D),
        spatial_qkv,
        spatial_out,
        mlp_up,
        mlp_down,
        temporal_qkv,
        temporal_out,
    )
    rows = rows.reshape(2, F, DP, D)
    return jnp.transpose(rows, (2, 1, 0, 3)).reshape(S, 1, 2, D)


def solution(mesh):
    placed = (
        P("dp", "mp", None),
        P("dp", "mp"),
        P(),
        P(None, None, "mp"),
        P("mp", None),
        P(),
        P(None, "mp"),
        P("mp", None),
        P(),
        P(),
        P(),
    )
    return jax.shard_map(
        local, mesh=mesh, in_specs=placed, out_specs=P(None, "mp", "dp", None), check_vma=False
    )
```

```python
import math

import jax
import jax.numpy as jnp
from jax import lax
from jax.experimental import pallas as pl
from jax.experimental.pallas import tpu as pltpu
from jax.sharding import PartitionSpec as P

HD = 64
PIX = 256
FRAMES = 12
EPS = 1e-06
F = 3
N = 256
H = 128
B = 64
D = 1024
C = 256
S = 96
DP = 32
BF = jnp.bfloat16
F32 = jnp.float32


def normalize(rows, gain):
    mean = jnp.sum(rows, axis=-1, keepdims=True) * (1.0 / D)
    centered = rows - mean
    spread = jnp.sum(centered * centered, axis=-1, keepdims=True) * (1.0 / D)
    return centered * lax.rsqrt(spread + EPS) * gain


def gelu(x):
    return 0.5 * x * (1.0 + lax.erf(x * (1.0 / math.sqrt(2.0))))


def at(start, size):
    return pl.ds(pl.multiple_of(start, size), size)


def dot(a, b):
    return jnp.dot(a, b, preferred_element_type=F32)


def dot_t(a, b):
    return lax.dot_general(a, b, (((1,), (1,)), ((), ())), preferred_element_type=F32)


def head_masks():
    lane = lax.broadcasted_iota(jnp.int32, (1, C), 1)
    return [(lane // HD == h) for h in range(C // HD)]


def attend(q, k, v, masks, shift):
    total = None
    for h in range(C // HD):
        scores = dot_t(jnp.where(masks[h], q, 0.0).astype(BF), k)
        if shift is not None:
            scores = scores + shift
        top = jnp.max(scores, axis=-1, keepdims=True)
        expo = jnp.exp(scores - top)
        denom = jnp.sum(expo, axis=-1, keepdims=True)
        mixed = dot(expo.astype(BF), v) * (1.0 / denom)
        total = mixed if h == 0 else jnp.where(masks[h], mixed, total)
    return total.astype(BF)


def kernel(
    tokens,
    counts,
    gain_one,
    gain_two,
    gain_three,
    w_qkv,
    w_out,
    w_up,
    w_down,
    t_qkv,
    t_out,
    out,
    tok,
    heads,
    mix,
    qkv_v,
    out_v,
    up_v,
    down_v,
    tqkv_v,
    tout_v,
    normed,
    q1,
    hidden,
    res,
    part,
    own,
    rx_send,
    rx_recv,
    cells,
    a_send,
    a_recv,
    c_send,
    c_recv,
    tcells,
    xs,
    n3,
    q2,
    m2,
    loc,
    tok_s,
    tok_r,
    mix_s,
    mix_r,
    rx_s,
    rx_r,
    a_s,
    a_r,
    w_s,
    w_r,
    rounds,
):
    dp = lax.axis_index("dp")
    mp = lax.axis_index("mp")
    core = mp % 2
    x_hi = mp // 2
    opp_i = (mp + 2) % 4
    sib = {"mp": mp + 1 - 2 * core}
    opp = {"mp": opp_i}
    diag = {"mp": (mp + 3 - 2 * core) % 4}
    cell = (dp // 8) * 4 + dp % 4
    x_lo = (dp // 4) % 2
    half = at(core * H, H)
    other = at((1 - core) * H, H)
    own_rows = at(core * H + x_hi * B, B)
    opp_rows = at(core * H + (1 - x_hi) * B, B)
    sib_rows = at((1 - core) * H + x_hi * B, B)
    diag_rows = at((1 - core) * H + (1 - x_hi) * B, B)
    in_half = at(x_hi * B, B)
    in_half_opp = at((1 - x_hi) * B, B)

    def remote(src, dst, ss, rs, where):
        return pltpu.make_async_remote_copy(
            src_ref=src, dst_ref=dst, send_sem=ss, recv_sem=rs, device_id=where
        )

    def local_copy(src, dst, i):
        return pltpu.make_async_copy(src, dst, loc.at[i])

    units = at(core * D, D)
    loads = [
        local_copy(tokens, tok.at[:, own_rows], 0),
        local_copy(w_qkv, qkv_v, 1),
        local_copy(w_out, out_v.at[at(mp * C, C)], 2),
        local_copy(w_up, up_v.at[core], 3),
        local_copy(w_down, down_v.at[units], 4),
        local_copy(t_qkv, tqkv_v, 5),
        local_copy(t_out, tout_v, 6),
    ]

    barrier = pltpu.get_barrier_semaphore()
    for i in range(1, 4):
        pl.semaphore_signal(barrier, inc=1, device_id={"mp": (mp + i) % 4})

    y, z = dp // 8, dp % 4
    near = [{"dp": (((y + i) % 4) * 2 + x_lo) * 4 + z} for i in (1, 2, 3)]
    near += [{"dp": dp - z + (z + i) % 4} for i in (1, 2, 3)]
    near += [{"dp": (y * 2 + 1 - x_lo) * 4 + z}]
    for who in near:
        pl.semaphore_signal(barrier, inc=1, device_id=who)
    loads[0].start()
    loads[1].start()
    pl.semaphore_wait(barrier, 3 + len(near))

    first = remote(
        w_out.at[at(cell * 16, 16)],
        out_v.at[at(mp * C + cell * 16, 16)],
        w_s.at[0],
        w_r.at[0],
        opp,
    )
    first.start()

    def tok_copy(f, kind):
        if kind < 2:
            return remote(
                tokens.at[f],
                tok.at[f, own_rows],
                tok_s.at[kind, f],
                tok_r.at[kind, f],
                opp if kind == 0 else sib,
            )
        blk = tok.at[f, opp_rows]
        return remote(blk, blk, tok_s.at[kind, f], tok_r.at[kind, f], sib)

    for f in range(F):
        tok_copy(f, 0).start()
    for f in range(F):
        tok_copy(f, 1).start()
    for who in near:
        pl.semaphore_signal(rounds.at[0], inc=1, device_id=who)
    for c in loads[2:5]:
        c.start()
    to_sib = [
        remote(w_out, out_v.at[at(mp * C, C)], w_s.at[1], w_r.at[1], sib),
        remote(w_up, up_v.at[core], w_s.at[4], w_r.at[4], sib),
        remote(w_down, down_v.at[units], w_s.at[5], w_r.at[5], sib),
    ]
    for c in to_sib:
        c.start()

    row = lax.broadcasted_iota(jnp.int32, (8, 128), 0)
    lane = lax.broadcasted_iota(jnp.int32, (8, 128), 1)

    @pl.loop(0, DP)
    def _(d):
        tile = jnp.zeros((8, 128), jnp.int32)
        for f in range(F):
            for p in range(2):
                spot = (row == p) & (lane == f * DP + dp)
                tile = jnp.where(spot, counts[f, d * 2 + p], tile)
        c_send[d] = tile.astype(F32)

    c_recv[dp] = c_send[dp]

    pl.semaphore_wait(rounds.at[0], len(near))
    for who in near:
        pl.semaphore_signal(rounds.at[1], inc=1, device_id=who)
    first.wait_recv()
    mine = at(opp_i * C + cell * 16, 16)

    @pl.loop(1, 16)
    def _(j):
        q = (cell + j) % 16
        to = ((q // 4) * 2 + x_lo) * 4 + q % 4
        remote(out_v.at[mine], out_v.at[mine], w_s.at[2], w_r.at[2], {"dp": to}).start()

    pl.semaphore_wait(rounds.at[1], len(near))

    @pl.loop(1, DP)
    def _(i):
        to = (dp + i) % DP
        remote(c_send.at[to], c_recv.at[dp], a_s.at[F], a_r.at[F], {"dp": to}).start()

    masks = head_masks()
    cols_mp = at(mp * C, C)

    def mix_copy(f, kind):
        src = heads.at[f, half if kind == 0 else other]
        dst = mix.at[f, :, cols_mp]
        return remote(
            src, dst, mix_s.at[kind, f], mix_r.at[kind, f], (opp, diag, sib)[kind]
        )

    def spatial_project(f, blocks):
        parts = [normalize(tok[f, b].astype(F32), gain_one[...]).astype(BF) for b in blocks]
        rows = jnp.concatenate(parts, axis=0)
        for i in range(3):
            value = dot(rows, qkv_v[i])
            if i == 0:
                value = value * (1.0 / math.sqrt(HD))
            value = value.astype(BF)
            for j, b in enumerate(blocks):
                q1[i, f, b] = value[j * B : (j + 1) * B]

    loads[0].wait()
    loads[1].wait()

    @pl.loop(0, F)
    def _(f):
        tok_copy(f, 1).wait_recv()
        spatial_project(f, (own_rows, sib_rows))

    @pl.loop(0, F)
    def _(f):
        tok_copy(f, 0).wait_recv()
        tok_copy(f, 2).start()
        tok_copy(f, 2).wait_recv()
        spatial_project(f, (opp_rows, diag_rows))
        heads[f] = attend(q1[0, f].astype(F32), q1[1, f], q1[2, f], masks, None)
        for kind in range(3):
            mix_copy(f, kind).start()
        mix[f, :, cols_mp] = heads[f, half]

    fifteen = out_v.at[pl.ds(0, 240)]
    remote(fifteen, fifteen, w_s.at[2], w_r.at[2], sib).wait_recv()
    block = out_v.at[at(opp_i * C, C)]
    pass_w = remote(block, block, w_s.at[3], w_r.at[3], sib)
    pass_w.start()
    for c in loads[5:]:
        c.start()
    for c in loads[2:5]:
        c.wait()
    for c in to_sib:
        c.wait_recv()
    pass_w.wait_recv()

    def rx_copy(f):
        return remote(rx_send.at[f], rx_recv.at[f], rx_s.at[f], rx_r.at[f], opp)

    @pl.loop(0, F)
    def _(f):
        for kind in range(3):
            mix_copy(f, kind).wait_recv()
        res[...] = dot(mix[f], out_v[...]) + tok[f, half].astype(F32)
        normed[...] = normalize(res[...], gain_two[...]).astype(BF)
        for j in range(2):
            for n in range(D // C):
                cols = pl.ds(n * C, C)
                hidden[:, pl.ds(j * D + n * C, C)] = gelu(
                    dot(normed[...], up_v[j, :, cols])
                ).astype(BF)
        part[...] = dot(hidden[...], down_v[...])
        rx_send[f] = part[in_half_opp].astype(BF)
        rx_copy(f).start()
        own[f] = res[in_half] + part[in_half]

    def parcels(f):
        rx_copy(f).wait_recv()
        value = own[f] + rx_recv[f].astype(F32)
        for c in range(8):
            cells[pl.ds(c, B, stride=8), :] = value[:, c * 128 : (c + 1) * 128]
        a_send[f] = cells[...].astype(BF).reshape(DP, 16, 128)
        a_recv[f, dp] = a_send[f, dp]

        @pl.loop(1, DP)
        def _(i):
            to = (dp + i) % DP
            remote(
                a_send.at[f, to], a_recv.at[f, dp], a_s.at[f], a_r.at[f], {"dp": to}
            ).start()

    for f in range(F):
        parcels(f)

    first.wait_send()
    for c in to_sib:
        c.wait_send()
    pass_w.wait_send()
    remote(fifteen, fifteen, w_s.at[2], w_r.at[2], sib).wait_send()
    for f in range(F):
        for kind in range(3):
            tok_copy(f, kind).wait_send()
            mix_copy(f, kind).wait_send()
        rx_copy(f).wait_send()

    loads[5].wait()
    loads[6].wait()
    most = c_send.at[pl.ds(0, DP - 1)]
    count_done = remote(most, most, a_s.at[F], a_r.at[F], opp)
    count_done.wait_send()
    count_done.wait_recv()
    seen = c_recv[0]
    for i in range(1, DP):
        seen = seen + c_recv[i]
    bias = jnp.log((seen + 1.0) / (PIX + 1.0))
    group = lax.broadcasted_iota(jnp.int32, (S, S), 0) % DP // (FRAMES // F)
    key_group = lax.broadcasted_iota(jnp.int32, (S, S), 1) % DP // (FRAMES // F)
    same = group == key_group

    def arrive(f):
        block = a_send.at[f, pl.ds(0, DP - 1)]
        done = remote(block, block, a_s.at[f], a_r.at[f], opp)
        done.wait_send()
        done.wait_recv()
        tcells[...] = a_recv[f].reshape(DP * 16, 128).astype(F32)
        for p in range(2):
            for c in range(8):
                xs[pl.ds(p * S + f * DP, DP), pl.ds(c * 128, 128)] = tcells[
                    pl.ds(p * 8 + c, DP, stride=16), :
                ]
            n3[pl.ds(f * 2 * DP + p * DP, DP)] = normalize(
                xs[pl.ds(p * S + f * DP, DP)], gain_three[...]
            ).astype(BF)

    def project(frames):
        rows = n3[pl.ds(frames[0] * 2 * DP, len(frames) * 2 * DP)]
        for i in range(3):
            for n in range(D // C):
                cols = pl.ds(n * C, C)
                value = dot(rows, tqkv_v[i, :, cols])
                if i == 0:
                    value = value * (1.0 / math.sqrt(HD))
                value = value.astype(BF)
                for j, f in enumerate(frames):
                    for p in range(2):
                        start = (j * 2 + p) * DP
                        q2[i, pl.ds(p * S + f * DP, DP), cols] = value[start : start + DP]

    arrive(0)
    project((0,))
    arrive(1)
    arrive(2)
    project((1, 2))

    for p in range(2):
        rows = pl.ds(p * S, S)
        shift = jnp.where(same, bias[p : p + 1, :S], -1e30)
        for n in range(D // C):
            cols = pl.ds(n * C, C)
            q = q2[0, rows, cols].astype(F32)
            m2[rows, cols] = attend(q, q2[1, rows, cols], q2[2, rows, cols], masks, shift)
    value = (xs[...] + dot(m2[...], tout_v[...])).astype(BF)
    out[...] = value.reshape(2, S, D)


def local(
    tokens,
    clear_count,
    gain_one,
    spatial_qkv,
    spatial_out,
    gain_two,
    mlp_up,
    mlp_down,
    gain_three,
    temporal_qkv,
    temporal_out,
):
    hbm = pl.BlockSpec(memory_space=pl.ANY)
    vmem = pl.BlockSpec(memory_space=pltpu.VMEM)
    smem = pl.BlockSpec(memory_space=pltpu.SMEM)
    dma = pltpu.SemaphoreType.DMA
    scratch = [
        pltpu.VMEM((F, N, D), BF),
        pltpu.VMEM((F, N, C), BF),
        pltpu.VMEM((F, H, D), BF),
        pltpu.VMEM((3, D, C), BF),
        pltpu.VMEM((D, D), BF),
        pltpu.VMEM((2, D, D), BF),
        pltpu.VMEM((2 * D, D), BF),
        pltpu.VMEM((3, D, D), BF),
        pltpu.VMEM((D, D), BF),
        pltpu.VMEM((H, D), BF),
        pltpu.VMEM((3, F, N, C), BF),
        pltpu.VMEM((H, 2 * D), BF),
        pltpu.VMEM((H, D), F32),
        pltpu.VMEM((H, D), F32),
        pltpu.VMEM((F, B, D), F32),
        pltpu.VMEM((F, B, D), BF),
        pltpu.VMEM((F, B, D), BF),
        pltpu.VMEM((B * 8, 128), F32),
        pltpu.VMEM((F, DP, 16, 128), BF),
        pltpu.VMEM((F, DP, 16, 128), BF),
        pltpu.VMEM((DP, 8, 128), F32),
        pltpu.VMEM((DP, 8, 128), F32),
        pltpu.VMEM((DP * 16, 128), F32),
        pltpu.VMEM((2 * S, D), F32),
        pltpu.VMEM((2 * S, D), BF),
        pltpu.VMEM((3, 2 * S, D), BF),
        pltpu.VMEM((2 * S, D), BF),
        dma((7,)),
        dma((3, F)),
        dma((3, F)),
        dma((3, F)),
        dma((3, F)),
        dma((F,)),
        dma((F,)),
        dma((F + 1,)),
        dma((F + 1,)),
        dma((6,)),
        dma((6,)),
        pltpu.SemaphoreType.REGULAR((2,)),
    ]
    rows = pl.pallas_call(
        kernel,
        out_shape=jax.ShapeDtypeStruct((2, S, D), BF),
        in_specs=[hbm, smem, vmem, vmem, vmem, hbm, hbm, hbm, hbm, hbm, hbm],
        out_specs=vmem,
        scratch_shapes=scratch,
        compiler_params=pltpu.CompilerParams(
            collective_id=0, has_side_effects=True, vmem_limit_bytes=60 * 1024 * 1024
        ),
        name="layers",
    )(
        tokens,
        clear_count,
        gain_one.reshape(1, D),
        gain_two.reshape(1, D),
        gain_three.reshape(1, D),
        spatial_qkv,
        spatial_out,
        mlp_up,
        mlp_down,
        temporal_qkv,
        temporal_out,
    )
    rows = rows.reshape(2, F, DP, D)
    return jnp.transpose(rows, (2, 1, 0, 3)).reshape(S, 1, 2, D)


def solution(mesh):
    placed = (
        P("dp", "mp", None),
        P("dp", "mp"),
        P(),
        P(None, None, "mp"),
        P("mp", None),
        P(),
        P(None, "mp"),
        P("mp", None),
        P(),
        P(),
        P(),
    )
    return jax.shard_map(
        local, mesh=mesh, in_specs=placed, out_specs=P(None, "mp", "dp", None), check_vma=False
    )
```

```python
import math

import jax
import jax.numpy as jnp
from jax import lax
from jax.experimental import pallas as pl
from jax.experimental.pallas import tpu as pltpu
from jax.sharding import PartitionSpec as P

HD = 64
PIX = 256
FRAMES = 12
EPS = 1e-06
F = 3
N = 256
H = 128
B = 64
D = 1024
C = 256
S = 96
DP = 32
BF = jnp.bfloat16
F32 = jnp.float32


def normalize(rows, gain):
    mean = jnp.sum(rows, axis=-1, keepdims=True) * (1.0 / D)
    centered = rows - mean
    spread = jnp.sum(centered * centered, axis=-1, keepdims=True) * (1.0 / D)
    return centered * lax.rsqrt(spread + EPS) * gain


def gelu(x):
    return 0.5 * x * (1.0 + lax.erf(x * (1.0 / math.sqrt(2.0))))


def at(start, size):
    return pl.ds(pl.multiple_of(start, size), size)


def dot(a, b):
    return jnp.dot(a, b, preferred_element_type=F32)


def dot_t(a, b):
    return lax.dot_general(a, b, (((1,), (1,)), ((), ())), preferred_element_type=F32)


def head_masks():
    lane = lax.broadcasted_iota(jnp.int32, (1, C), 1)
    return [(lane // HD == h) for h in range(C // HD)]


def attend(q, k, v, masks, shift):
    total = None
    for h in range(C // HD):
        scores = dot_t(jnp.where(masks[h], q, 0.0).astype(BF), k)
        if shift is not None:
            scores = scores + shift
        top = jnp.max(scores, axis=-1, keepdims=True)
        expo = jnp.exp(scores - top)
        denom = jnp.sum(expo, axis=-1, keepdims=True)
        mixed = dot(expo.astype(BF), v) * (1.0 / denom)
        total = mixed if h == 0 else jnp.where(masks[h], mixed, total)
    return total.astype(BF)


def kernel(
    tokens,
    counts,
    gain_one,
    gain_two,
    gain_three,
    w_qkv,
    w_out,
    w_up,
    w_down,
    t_qkv,
    t_out,
    out,
    tok,
    heads,
    mix,
    qkv_v,
    out_v,
    up_v,
    down_v,
    tqkv_v,
    tout_v,
    normed,
    q1,
    hidden,
    res,
    part,
    own,
    rx_send,
    rx_recv,
    cells,
    a_send,
    a_recv,
    c_send,
    c_recv,
    tcells,
    xs,
    n3,
    q2,
    m2,
    loc,
    tok_s,
    tok_r,
    mix_s,
    mix_r,
    rx_s,
    rx_r,
    a_s,
    a_r,
    w_s,
    w_r,
    rounds,
):
    dp = lax.axis_index("dp")
    mp = lax.axis_index("mp")
    core = mp % 2
    x_hi = mp // 2
    opp_i = (mp + 2) % 4
    sib = {"mp": mp + 1 - 2 * core}
    opp = {"mp": opp_i}
    diag = {"mp": (mp + 3 - 2 * core) % 4}
    cell = (dp // 8) * 4 + dp % 4
    x_lo = (dp // 4) % 2
    half = at(core * H, H)
    other = at((1 - core) * H, H)
    own_rows = at(core * H + x_hi * B, B)
    opp_rows = at(core * H + (1 - x_hi) * B, B)
    sib_rows = at((1 - core) * H + x_hi * B, B)
    diag_rows = at((1 - core) * H + (1 - x_hi) * B, B)
    in_half = at(x_hi * B, B)
    in_half_opp = at((1 - x_hi) * B, B)

    def remote(src, dst, ss, rs, where):
        return pltpu.make_async_remote_copy(
            src_ref=src, dst_ref=dst, send_sem=ss, recv_sem=rs, device_id=where
        )

    def local_copy(src, dst, i):
        return pltpu.make_async_copy(src, dst, loc.at[i])

    units = at(core * D, D)
    loads = [
        local_copy(tokens, tok.at[:, own_rows], 0),
        local_copy(w_qkv, qkv_v, 1),
        local_copy(w_out, out_v.at[at(mp * C, C)], 2),
        local_copy(w_up, up_v.at[core], 3),
        local_copy(w_down, down_v.at[units], 4),
        local_copy(t_qkv, tqkv_v, 5),
        local_copy(t_out, tout_v, 6),
    ]

    barrier = pltpu.get_barrier_semaphore()
    for i in range(1, 4):
        pl.semaphore_signal(barrier, inc=1, device_id={"mp": (mp + i) % 4})

    y, z = dp // 8, dp % 4
    near = [{"dp": (((y + i) % 4) * 2 + x_lo) * 4 + z} for i in (1, 2, 3)]
    near += [{"dp": dp - z + (z + i) % 4} for i in (1, 2, 3)]
    near += [{"dp": (y * 2 + 1 - x_lo) * 4 + z}]
    for who in near:
        pl.semaphore_signal(barrier, inc=1, device_id=who)
    loads[0].start()
    loads[1].start()
    pl.semaphore_wait(barrier, 3 + len(near))

    first = remote(
        w_out.at[at(cell * 16, 16)],
        out_v.at[at(mp * C + cell * 16, 16)],
        w_s.at[0],
        w_r.at[0],
        opp,
    )
    first.start()

    def tok_copy(f, kind):
        if kind < 2:
            return remote(
                tokens.at[f],
                tok.at[f, own_rows],
                tok_s.at[kind, f],
                tok_r.at[kind, f],
                opp if kind == 0 else sib,
            )
        blk = tok.at[f, opp_rows]
        return remote(blk, blk, tok_s.at[kind, f], tok_r.at[kind, f], sib)

    for f in range(F):
        tok_copy(f, 0).start()
    for f in range(F):
        tok_copy(f, 1).start()
    for who in near:
        pl.semaphore_signal(rounds.at[0], inc=1, device_id=who)
    for c in loads[2:5]:
        c.start()
    to_sib = [
        remote(w_out, out_v.at[at(mp * C, C)], w_s.at[1], w_r.at[1], sib),
        remote(w_up, up_v.at[core], w_s.at[4], w_r.at[4], sib),
        remote(w_down, down_v.at[units], w_s.at[5], w_r.at[5], sib),
    ]
    for c in to_sib:
        c.start()

    row = lax.broadcasted_iota(jnp.int32, (2, 128), 0)
    lane = lax.broadcasted_iota(jnp.int32, (2, 128), 1)

    @pl.loop(0, DP)
    def _(d):
        tile = jnp.zeros((2, 128), jnp.int32)
        for f in range(F):
            for p in range(2):
                spot = (row == p) & (lane == f * DP + dp)
                tile = jnp.where(spot, counts[f, d * 2 + p], tile)
        c_send[d] = tile.astype(F32)

    c_recv[dp] = c_send[dp]

    pl.semaphore_wait(rounds.at[0], len(near))
    for who in near:
        pl.semaphore_signal(rounds.at[1], inc=1, device_id=who)
    first.wait_recv()
    mine = at(opp_i * C + cell * 16, 16)

    @pl.loop(1, 16)
    def _(j):
        q = (cell + j) % 16
        to = ((q // 4) * 2 + x_lo) * 4 + q % 4
        remote(out_v.at[mine], out_v.at[mine], w_s.at[2], w_r.at[2], {"dp": to}).start()

    pl.semaphore_wait(rounds.at[1], len(near))

    @pl.loop(1, DP)
    def _(i):
        to = (dp + i) % DP
        remote(c_send.at[to], c_recv.at[dp], a_s.at[F], a_r.at[F], {"dp": to}).start()

    masks = head_masks()
    cols_mp = at(mp * C, C)

    def mix_copy(f, kind):
        src = heads.at[f, half if kind == 0 else other]
        dst = mix.at[f, :, cols_mp]
        return remote(
            src, dst, mix_s.at[kind, f], mix_r.at[kind, f], (opp, diag, sib)[kind]
        )

    def spatial_project(f, blocks):
        parts = [normalize(tok[f, b].astype(F32), gain_one[...]).astype(BF) for b in blocks]
        rows = jnp.concatenate(parts, axis=0)
        for i in range(3):
            value = dot(rows, qkv_v[i])
            if i == 0:
                value = value * (1.0 / math.sqrt(HD))
            value = value.astype(BF)
            for j, b in enumerate(blocks):
                q1[i, f, b] = value[j * B : (j + 1) * B]

    loads[0].wait()
    loads[1].wait()

    @pl.loop(0, F)
    def _(f):
        tok_copy(f, 1).wait_recv()
        spatial_project(f, (own_rows, sib_rows))

    @pl.loop(0, F)
    def _(f):
        tok_copy(f, 0).wait_recv()
        tok_copy(f, 2).start()
        tok_copy(f, 2).wait_recv()
        spatial_project(f, (opp_rows, diag_rows))
        heads[f] = attend(q1[0, f].astype(F32), q1[1, f], q1[2, f], masks, None)
        for kind in range(3):
            mix_copy(f, kind).start()
        mix[f, :, cols_mp] = heads[f, half]

    fifteen = out_v.at[pl.ds(0, 240)]
    remote(fifteen, fifteen, w_s.at[2], w_r.at[2], sib).wait_recv()
    block = out_v.at[at(opp_i * C, C)]
    pass_w = remote(block, block, w_s.at[3], w_r.at[3], sib)
    pass_w.start()
    for c in loads[5:]:
        c.start()
    for c in loads[2:5]:
        c.wait()
    for c in to_sib:
        c.wait_recv()
    pass_w.wait_recv()

    def rx_copy(f):
        return remote(rx_send.at[f], rx_recv.at[f], rx_s.at[f], rx_r.at[f], opp)

    @pl.loop(0, F)
    def _(f):
        for kind in range(3):
            mix_copy(f, kind).wait_recv()
        res[...] = dot(mix[f], out_v[...]) + tok[f, half].astype(F32)
        normed[...] = normalize(res[...], gain_two[...]).astype(BF)
        for j in range(2):
            for n in range(D // C):
                cols = pl.ds(n * C, C)
                hidden[:, pl.ds(j * D + n * C, C)] = gelu(
                    dot(normed[...], up_v[j, :, cols])
                ).astype(BF)
        part[...] = dot(hidden[...], down_v[...])
        rx_send[f] = part[in_half_opp].astype(BF)
        rx_copy(f).start()
        own[f] = res[in_half] + part[in_half]

    def parcels(f):
        rx_copy(f).wait_recv()
        value = own[f] + rx_recv[f].astype(F32)
        for c in range(8):
            cells[pl.ds(c, B, stride=8), :] = value[:, c * 128 : (c + 1) * 128]
        a_send[f] = cells[...].astype(BF).reshape(DP, 16, 128)
        a_recv[f, dp] = a_send[f, dp]

        @pl.loop(1, DP)
        def _(i):
            to = (dp + i) % DP
            remote(
                a_send.at[f, to], a_recv.at[f, dp], a_s.at[f], a_r.at[f], {"dp": to}
            ).start()

    for f in range(F):
        parcels(f)

    first.wait_send()
    for c in to_sib:
        c.wait_send()
    pass_w.wait_send()
    remote(fifteen, fifteen, w_s.at[2], w_r.at[2], sib).wait_send()
    for f in range(F):
        for kind in range(3):
            tok_copy(f, kind).wait_send()
            mix_copy(f, kind).wait_send()
        rx_copy(f).wait_send()

    loads[5].wait()
    loads[6].wait()
    most = c_send.at[pl.ds(0, DP - 1)]
    count_done = remote(most, most, a_s.at[F], a_r.at[F], opp)
    count_done.wait_send()
    count_done.wait_recv()
    seen = c_recv[0]
    for i in range(1, DP):
        seen = seen + c_recv[i]
    bias = jnp.log((seen + 1.0) / (PIX + 1.0))
    group = lax.broadcasted_iota(jnp.int32, (S, S), 0) % DP // (FRAMES // F)
    key_group = lax.broadcasted_iota(jnp.int32, (S, S), 1) % DP // (FRAMES // F)
    same = group == key_group

    def arrive(f):
        block = a_send.at[f, pl.ds(0, DP - 1)]
        done = remote(block, block, a_s.at[f], a_r.at[f], opp)
        done.wait_send()
        done.wait_recv()
        tcells[...] = a_recv[f].reshape(DP * 16, 128).astype(F32)
        for p in range(2):
            for c in range(8):
                xs[pl.ds(p * S + f * DP, DP), pl.ds(c * 128, 128)] = tcells[
                    pl.ds(p * 8 + c, DP, stride=16), :
                ]
            n3[pl.ds(f * 2 * DP + p * DP, DP)] = normalize(
                xs[pl.ds(p * S + f * DP, DP)], gain_three[...]
            ).astype(BF)

    def project(frames):
        rows = n3[pl.ds(frames[0] * 2 * DP, len(frames) * 2 * DP)]
        for i in range(3):
            for n in range(D // C):
                cols = pl.ds(n * C, C)
                value = dot(rows, tqkv_v[i, :, cols])
                if i == 0:
                    value = value * (1.0 / math.sqrt(HD))
                value = value.astype(BF)
                for j, f in enumerate(frames):
                    for p in range(2):
                        start = (j * 2 + p) * DP
                        q2[i, pl.ds(p * S + f * DP, DP), cols] = value[start : start + DP]

    arrive(0)
    project((0,))
    arrive(1)
    arrive(2)
    project((1, 2))

    for p in range(2):
        rows = pl.ds(p * S, S)
        shift = jnp.where(same, bias[p : p + 1, :S], -1e30)
        for n in range(D // C):
            cols = pl.ds(n * C, C)
            q = q2[0, rows, cols].astype(F32)
            m2[rows, cols] = attend(q, q2[1, rows, cols], q2[2, rows, cols], masks, shift)
    value = (xs[...] + dot(m2[...], tout_v[...])).astype(BF)
    out[...] = value.reshape(2, S, D)


def local(
    tokens,
    clear_count,
    gain_one,
    spatial_qkv,
    spatial_out,
    gain_two,
    mlp_up,
    mlp_down,
    gain_three,
    temporal_qkv,
    temporal_out,
):
    hbm = pl.BlockSpec(memory_space=pl.ANY)
    vmem = pl.BlockSpec(memory_space=pltpu.VMEM)
    smem = pl.BlockSpec(memory_space=pltpu.SMEM)
    dma = pltpu.SemaphoreType.DMA
    scratch = [
        pltpu.VMEM((F, N, D), BF),
        pltpu.VMEM((F, N, C), BF),
        pltpu.VMEM((F, H, D), BF),
        pltpu.VMEM((3, D, C), BF),
        pltpu.VMEM((D, D), BF),
        pltpu.VMEM((2, D, D), BF),
        pltpu.VMEM((2 * D, D), BF),
        pltpu.VMEM((3, D, D), BF),
        pltpu.VMEM((D, D), BF),
        pltpu.VMEM((H, D), BF),
        pltpu.VMEM((3, F, N, C), BF),
        pltpu.VMEM((H, 2 * D), BF),
        pltpu.VMEM((H, D), F32),
        pltpu.VMEM((H, D), F32),
        pltpu.VMEM((F, B, D), F32),
        pltpu.VMEM((F, B, D), BF),
        pltpu.VMEM((F, B, D), BF),
        pltpu.VMEM((B * 8, 128), F32),
        pltpu.VMEM((F, DP, 16, 128), BF),
        pltpu.VMEM((F, DP, 16, 128), BF),
        pltpu.VMEM((DP, 2, 128), F32),
        pltpu.VMEM((DP, 2, 128), F32),
        pltpu.VMEM((DP * 16, 128), F32),
        pltpu.VMEM((2 * S, D), F32),
        pltpu.VMEM((2 * S, D), BF),
        pltpu.VMEM((3, 2 * S, D), BF),
        pltpu.VMEM((2 * S, D), BF),
        dma((7,)),
        dma((3, F)),
        dma((3, F)),
        dma((3, F)),
        dma((3, F)),
        dma((F,)),
        dma((F,)),
        dma((F + 1,)),
        dma((F + 1,)),
        dma((6,)),
        dma((6,)),
        pltpu.SemaphoreType.REGULAR((2,)),
    ]
    rows = pl.pallas_call(
        kernel,
        out_shape=jax.ShapeDtypeStruct((2, S, D), BF),
        in_specs=[hbm, smem, vmem, vmem, vmem, hbm, hbm, hbm, hbm, hbm, hbm],
        out_specs=vmem,
        scratch_shapes=scratch,
        compiler_params=pltpu.CompilerParams(
            collective_id=0, has_side_effects=True, vmem_limit_bytes=60 * 1024 * 1024
        ),
        name="layers",
    )(
        tokens,
        clear_count,
        gain_one.reshape(1, D),
        gain_two.reshape(1, D),
        gain_three.reshape(1, D),
        spatial_qkv,
        spatial_out,
        mlp_up,
        mlp_down,
        temporal_qkv,
        temporal_out,
    )
    rows = rows.reshape(2, F, DP, D)
    return jnp.transpose(rows, (2, 1, 0, 3)).reshape(S, 1, 2, D)


def solution(mesh):
    placed = (
        P("dp", "mp", None),
        P("dp", "mp"),
        P(),
        P(None, None, "mp"),
        P("mp", None),
        P(),
        P(None, "mp"),
        P("mp", None),
        P(),
        P(),
        P(),
    )
    return jax.shard_map(
        local, mesh=mesh, in_specs=placed, out_specs=P(None, "mp", "dp", None), check_vma=False
    )
```

```python
import math

import jax
import jax.numpy as jnp
from jax import lax
from jax.experimental import pallas as pl
from jax.experimental.pallas import tpu as pltpu
from jax.sharding import PartitionSpec as P

HD = 64
PIX = 256
FRAMES = 12
EPS = 1e-06
F = 3
N = 256
H = 128
B = 64
D = 1024
C = 256
S = 96
DP = 32
BF = jnp.bfloat16
F32 = jnp.float32


def normalize(rows, gain):
    mean = jnp.sum(rows, axis=-1, keepdims=True) * (1.0 / D)
    centered = rows - mean
    spread = jnp.sum(centered * centered, axis=-1, keepdims=True) * (1.0 / D)
    return centered * lax.rsqrt(spread + EPS) * gain


def gelu(x):
    return 0.5 * x * (1.0 + lax.erf(x * (1.0 / math.sqrt(2.0))))


def at(start, size):
    return pl.ds(pl.multiple_of(start, size), size)


def dot(a, b):
    return jnp.dot(a, b, preferred_element_type=F32)


def dot_t(a, b):
    return lax.dot_general(a, b, (((1,), (1,)), ((), ())), preferred_element_type=F32)


def head_masks():
    lane = lax.broadcasted_iota(jnp.int32, (1, C), 1)
    return [(lane // HD == h) for h in range(C // HD)]


def attend(q, k, v, masks, shift):
    total = None
    for h in range(C // HD):
        scores = dot_t(jnp.where(masks[h], q, 0.0).astype(BF), k)
        if shift is not None:
            scores = scores + shift
        top = jnp.max(scores, axis=-1, keepdims=True)
        expo = jnp.exp(scores - top)
        denom = jnp.sum(expo, axis=-1, keepdims=True)
        mixed = dot(expo.astype(BF), v) * (1.0 / denom)
        total = mixed if h == 0 else jnp.where(masks[h], mixed, total)
    return total.astype(BF)


def kernel(
    tokens,
    counts,
    gain_one,
    gain_two,
    gain_three,
    w_qkv,
    w_out,
    w_up,
    w_down,
    t_qkv,
    t_out,
    out,
    tok,
    heads,
    mix,
    qkv_v,
    out_v,
    up_v,
    down_v,
    tqkv_v,
    tout_v,
    normed,
    q1,
    hidden,
    pre,
    res,
    part,
    own,
    rx_send,
    rx_recv,
    cells,
    a_send,
    a_recv,
    c_send,
    c_recv,
    tcells,
    xs,
    n3,
    q2,
    m2,
    loc,
    tok_s,
    tok_r,
    mix_s,
    mix_r,
    rx_s,
    rx_r,
    a_s,
    a_r,
    w_s,
    w_r,
    rounds,
):
    dp = lax.axis_index("dp")
    mp = lax.axis_index("mp")
    core = mp % 2
    x_hi = mp // 2
    opp_i = (mp + 2) % 4
    sib = {"mp": mp + 1 - 2 * core}
    opp = {"mp": opp_i}
    diag = {"mp": (mp + 3 - 2 * core) % 4}
    cell = (dp // 8) * 4 + dp % 4
    x_lo = (dp // 4) % 2
    half = at(core * H, H)
    other = at((1 - core) * H, H)
    own_rows = at(core * H + x_hi * B, B)
    opp_rows = at(core * H + (1 - x_hi) * B, B)
    sib_rows = at((1 - core) * H + x_hi * B, B)
    diag_rows = at((1 - core) * H + (1 - x_hi) * B, B)
    in_half = at(x_hi * B, B)
    in_half_opp = at((1 - x_hi) * B, B)

    def remote(src, dst, ss, rs, where):
        return pltpu.make_async_remote_copy(
            src_ref=src, dst_ref=dst, send_sem=ss, recv_sem=rs, device_id=where
        )

    def local_copy(src, dst, i):
        return pltpu.make_async_copy(src, dst, loc.at[i])

    units = at(core * D, D)
    loads = [
        local_copy(tokens, tok.at[:, own_rows], 0),
        local_copy(w_qkv, qkv_v, 1),
        local_copy(w_out, out_v.at[at(mp * C, C)], 2),
        local_copy(w_up, up_v.at[core], 3),
        local_copy(w_down, down_v.at[units], 4),
        local_copy(t_qkv, tqkv_v, 5),
        local_copy(t_out, tout_v, 6),
    ]

    barrier = pltpu.get_barrier_semaphore()
    for i in range(1, 4):
        pl.semaphore_signal(barrier, inc=1, device_id={"mp": (mp + i) % 4})

    y, z = dp // 8, dp % 4
    near = [{"dp": (((y + i) % 4) * 2 + x_lo) * 4 + z} for i in (1, 2, 3)]
    near += [{"dp": dp - z + (z + i) % 4} for i in (1, 2, 3)]
    near += [{"dp": (y * 2 + 1 - x_lo) * 4 + z}]
    for who in near:
        pl.semaphore_signal(barrier, inc=1, device_id=who)
    loads[0].start()
    loads[1].start()
    pl.semaphore_wait(barrier, 3 + len(near))

    first = remote(
        w_out.at[at(cell * 16, 16)],
        out_v.at[at(mp * C + cell * 16, 16)],
        w_s.at[0],
        w_r.at[0],
        opp,
    )
    first.start()

    def tok_copy(f, kind):
        if kind < 2:
            return remote(
                tokens.at[f],
                tok.at[f, own_rows],
                tok_s.at[kind, f],
                tok_r.at[kind, f],
                opp if kind == 0 else sib,
            )
        blk = tok.at[f, opp_rows]
        return remote(blk, blk, tok_s.at[kind, f], tok_r.at[kind, f], sib)

    for f in range(F):
        tok_copy(f, 0).start()
    for f in range(F):
        tok_copy(f, 1).start()
    for who in near:
        pl.semaphore_signal(rounds.at[0], inc=1, device_id=who)
    for c in loads[2:5]:
        c.start()
    to_sib = [
        remote(w_out, out_v.at[at(mp * C, C)], w_s.at[1], w_r.at[1], sib),
        remote(w_up, up_v.at[core], w_s.at[4], w_r.at[4], sib),
        remote(w_down, down_v.at[units], w_s.at[5], w_r.at[5], sib),
    ]
    for c in to_sib:
        c.start()

    row = lax.broadcasted_iota(jnp.int32, (2, 128), 0)
    lane = lax.broadcasted_iota(jnp.int32, (2, 128), 1)

    @pl.loop(0, DP)
    def _(d):
        tile = jnp.zeros((2, 128), jnp.int32)
        for f in range(F):
            for p in range(2):
                spot = (row == p) & (lane == f * DP + dp)
                tile = jnp.where(spot, counts[f, d * 2 + p], tile)
        c_send[d] = tile.astype(F32)

    c_recv[dp] = c_send[dp]

    pl.semaphore_wait(rounds.at[0], len(near))
    for who in near:
        pl.semaphore_signal(rounds.at[1], inc=1, device_id=who)
    first.wait_recv()
    mine = at(opp_i * C + cell * 16, 16)

    @pl.loop(1, 16)
    def _(j):
        q = (cell + j) % 16
        to = ((q // 4) * 2 + x_lo) * 4 + q % 4
        remote(out_v.at[mine], out_v.at[mine], w_s.at[2], w_r.at[2], {"dp": to}).start()

    pl.semaphore_wait(rounds.at[1], len(near))

    @pl.loop(1, DP)
    def _(i):
        to = (dp + i) % DP
        remote(c_send.at[to], c_recv.at[dp], a_s.at[F], a_r.at[F], {"dp": to}).start()

    masks = head_masks()
    cols_mp = at(mp * C, C)

    def mix_copy(f, kind):
        src = heads.at[f, half if kind == 0 else other]
        dst = mix.at[f, :, cols_mp]
        return remote(
            src, dst, mix_s.at[kind, f], mix_r.at[kind, f], (opp, diag, sib)[kind]
        )

    def spatial_project(f, blocks):
        parts = [normalize(tok[f, b].astype(F32), gain_one[...]).astype(BF) for b in blocks]
        rows = jnp.concatenate(parts, axis=0)
        for i in range(3):
            value = dot(rows, qkv_v[i])
            if i == 0:
                value = value * (1.0 / math.sqrt(HD))
            value = value.astype(BF)
            for j, b in enumerate(blocks):
                q1[i, f, b] = value[j * B : (j + 1) * B]

    loads[0].wait()
    loads[1].wait()

    @pl.loop(0, F)
    def _(f):
        tok_copy(f, 1).wait_recv()
        spatial_project(f, (own_rows, sib_rows))

    @pl.loop(0, F)
    def _(f):
        tok_copy(f, 0).wait_recv()
        tok_copy(f, 2).start()
        tok_copy(f, 2).wait_recv()
        spatial_project(f, (opp_rows, diag_rows))
        heads[f] = attend(q1[0, f].astype(F32), q1[1, f], q1[2, f], masks, None)
        for kind in range(3):
            mix_copy(f, kind).start()
        mix[f, :, cols_mp] = heads[f, half]

    fifteen = out_v.at[pl.ds(0, 240)]
    remote(fifteen, fifteen, w_s.at[2], w_r.at[2], sib).wait_recv()
    block = out_v.at[at(opp_i * C, C)]
    pass_w = remote(block, block, w_s.at[3], w_r.at[3], sib)
    pass_w.start()
    for c in loads[5:]:
        c.start()
    for c in loads[2:5]:
        c.wait()
    for c in to_sib:
        c.wait_recv()
    chip = at(x_hi * 2 * C, 2 * C)
    away = at((1 - x_hi) * 2 * C, 2 * C)
    for f in range(F):
        mix_copy(f, 2).wait_recv()
        pre[f] = dot(mix[f, :, chip], out_v[chip]) + tok[f, half].astype(F32)
    pass_w.wait_recv()

    def rx_copy(f):
        return remote(rx_send.at[f], rx_recv.at[f], rx_s.at[f], rx_r.at[f], opp)

    @pl.loop(0, F)
    def _(f):
        for kind in range(2):
            mix_copy(f, kind).wait_recv()
        res[...] = pre[f] + dot(mix[f, :, away], out_v[away])
        normed[...] = normalize(res[...], gain_two[...]).astype(BF)
        for j in range(2):
            for n in range(D // C):
                cols = pl.ds(n * C, C)
                hidden[:, pl.ds(j * D + n * C, C)] = gelu(
                    dot(normed[...], up_v[j, :, cols])
                ).astype(BF)
        part[...] = dot(hidden[...], down_v[...])
        rx_send[f] = part[in_half_opp].astype(BF)
        rx_copy(f).start()
        own[f] = res[in_half] + part[in_half]

    def parcels(f):
        rx_copy(f).wait_recv()
        value = own[f] + rx_recv[f].astype(F32)
        for c in range(8):
            cells[pl.ds(c, B, stride=8), :] = value[:, c * 128 : (c + 1) * 128]
        a_send[f] = cells[...].astype(BF).reshape(DP, 16, 128)
        a_recv[f, dp] = a_send[f, dp]

        @pl.loop(1, DP)
        def _(i):
            to = (dp + i) % DP
            remote(
                a_send.at[f, to], a_recv.at[f, dp], a_s.at[f], a_r.at[f], {"dp": to}
            ).start()

    for f in range(F):
        parcels(f)

    first.wait_send()
    for c in to_sib:
        c.wait_send()
    pass_w.wait_send()
    remote(fifteen, fifteen, w_s.at[2], w_r.at[2], sib).wait_send()
    for f in range(F):
        for kind in range(3):
            tok_copy(f, kind).wait_send()
            mix_copy(f, kind).wait_send()
        rx_copy(f).wait_send()

    loads[5].wait()
    loads[6].wait()
    most = c_send.at[pl.ds(0, DP - 1)]
    count_done = remote(most, most, a_s.at[F], a_r.at[F], opp)
    count_done.wait_send()
    count_done.wait_recv()
    seen = c_recv[0]
    for i in range(1, DP):
        seen = seen + c_recv[i]
    bias = jnp.log((seen + 1.0) / (PIX + 1.0))
    group = lax.broadcasted_iota(jnp.int32, (S, S), 0) % DP // (FRAMES // F)
    key_group = lax.broadcasted_iota(jnp.int32, (S, S), 1) % DP // (FRAMES // F)
    same = group == key_group

    def arrive(f):
        block = a_send.at[f, pl.ds(0, DP - 1)]
        done = remote(block, block, a_s.at[f], a_r.at[f], opp)
        done.wait_send()
        done.wait_recv()
        tcells[...] = a_recv[f].reshape(DP * 16, 128).astype(F32)
        for p in range(2):
            for c in range(8):
                xs[pl.ds(p * S + f * DP, DP), pl.ds(c * 128, 128)] = tcells[
                    pl.ds(p * 8 + c, DP, stride=16), :
                ]
            n3[pl.ds(f * 2 * DP + p * DP, DP)] = normalize(
                xs[pl.ds(p * S + f * DP, DP)], gain_three[...]
            ).astype(BF)

    def project(frames):
        rows = n3[pl.ds(frames[0] * 2 * DP, len(frames) * 2 * DP)]
        for i in range(3):
            for n in range(D // C):
                cols = pl.ds(n * C, C)
                value = dot(rows, tqkv_v[i, :, cols])
                if i == 0:
                    value = value * (1.0 / math.sqrt(HD))
                value = value.astype(BF)
                for j, f in enumerate(frames):
                    for p in range(2):
                        start = (j * 2 + p) * DP
                        q2[i, pl.ds(p * S + f * DP, DP), cols] = value[start : start + DP]

    arrive(0)
    project((0,))
    arrive(1)
    arrive(2)
    project((1, 2))

    for p in range(2):
        rows = pl.ds(p * S, S)
        shift = jnp.where(same, bias[p : p + 1, :S], -1e30)
        for n in range(D // C):
            cols = pl.ds(n * C, C)
            q = q2[0, rows, cols].astype(F32)
            m2[rows, cols] = attend(q, q2[1, rows, cols], q2[2, rows, cols], masks, shift)
    value = (xs[...] + dot(m2[...], tout_v[...])).astype(BF)
    out[...] = value.reshape(2, S, D)


def local(
    tokens,
    clear_count,
    gain_one,
    spatial_qkv,
    spatial_out,
    gain_two,
    mlp_up,
    mlp_down,
    gain_three,
    temporal_qkv,
    temporal_out,
):
    hbm = pl.BlockSpec(memory_space=pl.ANY)
    vmem = pl.BlockSpec(memory_space=pltpu.VMEM)
    smem = pl.BlockSpec(memory_space=pltpu.SMEM)
    dma = pltpu.SemaphoreType.DMA
    scratch = [
        pltpu.VMEM((F, N, D), BF),
        pltpu.VMEM((F, N, C), BF),
        pltpu.VMEM((F, H, D), BF),
        pltpu.VMEM((3, D, C), BF),
        pltpu.VMEM((D, D), BF),
        pltpu.VMEM((2, D, D), BF),
        pltpu.VMEM((2 * D, D), BF),
        pltpu.VMEM((3, D, D), BF),
        pltpu.VMEM((D, D), BF),
        pltpu.VMEM((H, D), BF),
        pltpu.VMEM((3, F, N, C), BF),
        pltpu.VMEM((H, 2 * D), BF),
        pltpu.VMEM((F, H, D), F32),
        pltpu.VMEM((H, D), F32),
        pltpu.VMEM((H, D), F32),
        pltpu.VMEM((F, B, D), F32),
        pltpu.VMEM((F, B, D), BF),
        pltpu.VMEM((F, B, D), BF),
        pltpu.VMEM((B * 8, 128), F32),
        pltpu.VMEM((F, DP, 16, 128), BF),
        pltpu.VMEM((F, DP, 16, 128), BF),
        pltpu.VMEM((DP, 2, 128), F32),
        pltpu.VMEM((DP, 2, 128), F32),
        pltpu.VMEM((DP * 16, 128), F32),
        pltpu.VMEM((2 * S, D), F32),
        pltpu.VMEM((2 * S, D), BF),
        pltpu.VMEM((3, 2 * S, D), BF),
        pltpu.VMEM((2 * S, D), BF),
        dma((7,)),
        dma((3, F)),
        dma((3, F)),
        dma((3, F)),
        dma((3, F)),
        dma((F,)),
        dma((F,)),
        dma((F + 1,)),
        dma((F + 1,)),
        dma((6,)),
        dma((6,)),
        pltpu.SemaphoreType.REGULAR((2,)),
    ]
    rows = pl.pallas_call(
        kernel,
        out_shape=jax.ShapeDtypeStruct((2, S, D), BF),
        in_specs=[hbm, smem, vmem, vmem, vmem, hbm, hbm, hbm, hbm, hbm, hbm],
        out_specs=vmem,
        scratch_shapes=scratch,
        compiler_params=pltpu.CompilerParams(
            collective_id=0, has_side_effects=True, vmem_limit_bytes=60 * 1024 * 1024
        ),
        name="layers",
    )(
        tokens,
        clear_count,
        gain_one.reshape(1, D),
        gain_two.reshape(1, D),
        gain_three.reshape(1, D),
        spatial_qkv,
        spatial_out,
        mlp_up,
        mlp_down,
        temporal_qkv,
        temporal_out,
    )
    rows = rows.reshape(2, F, DP, D)
    return jnp.transpose(rows, (2, 1, 0, 3)).reshape(S, 1, 2, D)


def solution(mesh):
    placed = (
        P("dp", "mp", None),
        P("dp", "mp"),
        P(),
        P(None, None, "mp"),
        P("mp", None),
        P(),
        P(None, "mp"),
        P("mp", None),
        P(),
        P(),
        P(),
    )
    return jax.shard_map(
        local, mesh=mesh, in_specs=placed, out_specs=P(None, "mp", "dp", None), check_vma=False
    )
```
